512 devices in a mesh: grp: 4 (over x_hi, core), lat: 16 (over z, x_lo), lon: 8 (over y).
Axes of the slice: x: 4 (x_hi: 2, x_lo: 2; x = x_hi * 2 + x_lo), y: 8, z: 8, core: 2. Of those that a mesh axis runs over, the one named last changes fastest.
Arguments:
- aloft_gridpoint: bfloat16 [8, 128, 2592], P('grp', 'lat', 'lon'), may hold values from -6 to 6
- parallel_nodes: int32 [128], P('lat'), may hold values from 20 to 2592, as said below
- layer_pressure_share: float32 [8], P('grp'), may hold values from 0.1 to 1
- layer_sensitivity: float32 [8], P('grp'), may hold values from 0.05 to 0.5
- associated_polynomial_quadrature: bfloat16 [128, 640, 1280], P('lat', 'lon'), may hold values from -0.75 to 0.75
- marine_heat: float32 [16, 512, 1024], P('grp', 'lat', 'lon'), may hold values from -6 to 6
- water_indicator: int32 [512, 1024], P('lat', 'lon'), may hold values 0 or 1
- heat_feeding_panels: int32 [512, 8, 4], P('lat', 'lon'), may hold values from 0 to 55295
- heat_transfer_factors: bfloat16 [512, 8, 4, 6, 128], P('lat', 'lon'), may hold values from -1.25 to 1.25
- skin_warmth_feeding_panels: int32 [128, 432, 2], P('lat', 'lon'), may hold values from 0 to 4095
- skin_warmth_mapping_factors: bfloat16 [128, 432, 2, 6, 128], P('lat', 'lon'), may hold values from -0.375 to 0.375
Outputs:
- spectra: float32 [1280, 16, 640], P('lat', 'grp', 'lon')
- ocean_out: float32 [16, 512, 1024], P('grp', 'lat', 'lon')
The draws below stay inside these ranges and needn't reach their ends.
Inputs may be any that keep to these rules, and one draw needn't show every extreme that they name: `parallel_nodes`: octahedral point counts 20 + 4 * min(g, G - 1 - g) of rising global latitudes g of a grid of G = 1288 latitudes, one latitude from each run of G // 128 of them; the first row is a polar one and one row lies at the equator.
All inputs are finite; a program needn't handle non-finite values. No bound on the sum of `water_indicator` on one device may be relied on, other than what follows from the above.
Results may differ from the reference program's by a relative error of at most 0.0046.
Values may be sent and summed in bfloat16 or wider, within the bound.
A program may use at most 128 MiB of HBM per device.

```python
import math
import jax
import jax.numpy as jnp
from jax import lax

MERIDIAN_TOTAL = 2592
M = 640
NDEG = 1280
AIR_PANEL_PLACES = 6
SEA_PANEL_PLACES = 128
K1 = 4
SEA_PANELS_IN_2 = 2
PARALLEL_TOTAL = 128
LEV = 8
OLEV = 16
OROWS = 512
OCOLS = 1024
ABLK = 55296
SEA_PANEL_TOTAL = 4096
N_LON = 8


def draw_parallel_nodes(key, part):
    key = jax.random.fold_in(key, 11)
    total_lats = (MERIDIAN_TOTAL - 16) // 2
    half_lats = total_lats // 2
    run_width = total_lats // PARALLEL_TOTAL
    rows = jnp.arange(PARALLEL_TOTAL, dtype=jnp.int32)
    offsets = jax.random.randint(key, (PARALLEL_TOTAL,), 0, run_width).astype(jnp.int32)
    offsets = jnp.where(rows == 0, 0, offsets)
    equator_row = (half_lats - 1) // run_width
    offsets = jnp.where(rows == equator_row, (half_lats - 1) % run_width, offsets)
    global_lat = run_width * rows + offsets
    counts = 20 + 4 * jnp.minimum(global_lat, total_lats - 1 - global_lat)
    return counts.astype(jnp.int32)


def touch_ends(result, rng, low, top_value):
    spot = [jax.random.randint(jax.random.fold_in(rng, axis), (), 0, length) for axis, length in enumerate(result.shape)]
    longest = result.shape.index(max(result.shape))
    neighbour = spot[:longest] + [(spot[longest] + 1) % result.shape[longest]] + spot[longest + 1:]
    return result.at[tuple(spot)].set(low).at[tuple(neighbour)].set(top_value)


def strengthened(entries, rng, source, target, shards_of, factor):
    owner, partner = [(jnp.arange(entries.shape[dim]) // (entries.shape[dim] // shards_of)).reshape([-1 if axis == dim else 1 for axis in range(entries.ndim)]) for dim in (source, target)]
    chosen = jax.random.permutation(rng, shards_of)[partner]
    strong = (owner == chosen) | (owner == (partner + shards_of // 2) % shards_of)
    return jnp.where(strong, factor * entries, entries)


def level_of(key, dims, split, low, top_value):
    factor_of = 1.0
    for axis_at, parts in split:
        heights = jax.random.uniform(jax.random.fold_in(jax.random.fold_in(key, 6), axis_at), (parts,), jnp.float32, low / len(split), top_value / len(split))
        factor_of = factor_of * jnp.repeat(jnp.exp(heights), dims[axis_at] // parts).reshape((-1,) + (1,) * (len(dims) - 1 - axis_at))
    return factor_of


def normal_values(own_key, shape, scale, limit, shards=(), kind=jnp.bfloat16):
    values = scale * jax.random.normal(own_key, shape, jnp.float32)
    if shards:
        values = values * level_of(own_key, shape, shards, -0.22, 0.18)
    return jnp.clip(values, -limit, limit).astype(kind)


def bell_draw_with(rng, extent, scale, reach, cuts, heavy, held_as=jnp.bfloat16):
    values = scale * jax.random.normal(rng, extent, jnp.float32)
    if cuts:
        values = values * level_of(rng, extent, cuts, -0.22, 0.18)
    return jnp.clip(strengthened(values, jax.random.fold_in(rng, 3), *heavy), -reach, reach).astype(held_as)


def setup_inputs(seed: int = 0) -> dict:
    seeds = jax.random.split(jax.random.key(seed), 12)
    return {
        "aloft_gridpoint": normal_values(seeds[0], (LEV, PARALLEL_TOTAL, MERIDIAN_TOTAL), 1.0, 6.0, ((0, 4), (1, 16), (2, 8))),
        "parallel_nodes": draw_parallel_nodes(jax.random.fold_in(seeds[11], 71), 0),
        "layer_pressure_share": jnp.clip(jnp.exp(math.log(1.0) - 2.3025851 * jax.random.uniform(seeds[2], (LEV,), jnp.float32) ** level_of(seeds[2], (LEV,), ((0, 4),), -0.2, 0.2)), 0.1, 1.0),
        "layer_sensitivity": jnp.clip(jnp.exp(math.log(0.5) - 2.3025851 * jax.random.uniform(seeds[3], (LEV,), jnp.float32) ** level_of(seeds[3], (LEV,), ((0, 4),), -0.2, 0.2)), 0.05, 0.5),
        "associated_polynomial_quadrature": bell_draw_with(seeds[4], (PARALLEL_TOTAL, M, NDEG), PARALLEL_TOTAL ** -0.5, 0.75, ((0, 16), (1, 8)), (0, 2, 16, 2.0)),
        "marine_heat": normal_values(seeds[5], (OLEV, OROWS, OCOLS), 1.0, 6.0, ((0, 4), (1, 16), (2, 8)), jnp.float32),
        "water_indicator": touch_ends((jax.random.randint(seeds[6], (OROWS, OCOLS), 0, 4) < 3).astype(jnp.int32), jax.random.fold_in(seeds[6], 1), 0, 1),
        "heat_feeding_panels": touch_ends(jax.random.randint(seeds[7], (OROWS, OCOLS // SEA_PANEL_PLACES, K1), 0, ABLK), jax.random.fold_in(seeds[7], 1), 0, ABLK - 1).astype(jnp.int32),
        "heat_transfer_factors": normal_values(seeds[8], (OROWS, OCOLS // SEA_PANEL_PLACES, K1, AIR_PANEL_PLACES, SEA_PANEL_PLACES), (K1 * AIR_PANEL_PLACES) ** -0.5, 1.25, ((0, 16), (1, 8))),
        "skin_warmth_feeding_panels": touch_ends(jax.random.randint(seeds[9], (PARALLEL_TOTAL, MERIDIAN_TOTAL // AIR_PANEL_PLACES, SEA_PANELS_IN_2), 0, SEA_PANEL_TOTAL), jax.random.fold_in(seeds[9], 1), 0, SEA_PANEL_TOTAL - 1).astype(jnp.int32),
        "skin_warmth_mapping_factors": normal_values(seeds[10], (PARALLEL_TOTAL, MERIDIAN_TOTAL // AIR_PANEL_PLACES, SEA_PANELS_IN_2, AIR_PANEL_PLACES, SEA_PANEL_PLACES), (SEA_PANELS_IN_2 * SEA_PANEL_PLACES) ** -0.5, 0.375, ((0, 16), (1, 8))),
    }


TWO_PI = 6.283185307179586
FLUX_RATE = 0.5
KAPPA = 0.2


def fourier_rows(values, count_pts, lon_ids, k_start, count):
    wave_ids = k_start + jnp.arange(count, dtype=jnp.int32)
    phases = (lon_ids[:, None] * wave_ids[None, :]) % count_pts
    angles = phases.astype(jnp.float32) * (TWO_PI / count_pts.astype(jnp.float32))
    usable = (lon_ids[:, None] < count_pts) & (2 * wave_ids[None, :] < count_pts)
    cosine = jnp.where(usable, jnp.cos(angles), 0.0).astype(jnp.bfloat16)
    sine = jnp.where(usable, -jnp.sin(angles), 0.0).astype(jnp.bfloat16)
    basis = jnp.concatenate([cosine, sine], axis=1)
    summed = jnp.dot(values, basis, preferred_element_type=jnp.float32) / count_pts.astype(jnp.float32)
    return summed.reshape(values.shape[0], 2, count).transpose(2, 0, 1)


def diffuse(field, wet):
    middle = field[:, 1:-1, 1:-1]
    wet_mid = wet[1:-1, 1:-1]
    total = jnp.zeros_like(middle)
    pairs = ((field[:, :-2, 1:-1], wet[:-2, 1:-1]), (field[:, 2:, 1:-1], wet[2:, 1:-1]),
             (field[:, 1:-1, :-2], wet[1:-1, :-2]), (field[:, 1:-1, 2:], wet[1:-1, 2:]))
    for near_field, near_wet in pairs:
        total = total + near_wet * (near_field - middle)
    return middle + KAPPA * wet_mid * total


def reference(aloft_gridpoint, parallel_nodes, layer_pressure_share, layer_sensitivity, associated_polynomial_quadrature, marine_heat, water_indicator, heat_feeding_panels, heat_transfer_factors, skin_warmth_feeding_panels, skin_warmth_mapping_factors):
    maximal_magnitude = lax.Precision.HIGHEST
    lon_ids = jnp.arange(MERIDIAN_TOTAL, dtype=jnp.int32)
    live = (lon_ids[None, :] < parallel_nodes[:, None]).astype(jnp.float32)
    aloft_state = aloft_gridpoint.astype(jnp.float32)
    column_flux = jnp.sum(layer_pressure_share[:, None, None] * aloft_state, axis=0) * live
    marine_panel_indices = marine_heat[0].reshape(-1, SEA_PANEL_PLACES)
    selected_elements = marine_panel_indices[skin_warmth_feeding_panels]
    marine_warmth = jnp.einsum("cmzqy,cmzy->cmq", skin_warmth_mapping_factors.astype(jnp.float32), selected_elements, precision=maximal_magnitude).reshape(PARALLEL_TOTAL, MERIDIAN_TOTAL)
    driven_tendency = (aloft_state + layer_sensitivity[:, None, None] * marine_warmth[None]).astype(jnp.bfloat16)

    def one_lat(pair):
        return fourier_rows(pair[0], pair[1], lon_ids, 0, M)

    waves = lax.map(one_lat, (driven_tendency.transpose(1, 0, 2), parallel_nodes))
    fourier = waves.transpose(1, 0, 2, 3).reshape(M, PARALLEL_TOTAL, LEV * 2).astype(jnp.bfloat16)

    block_width = M // N_LON
    basis_blocks = associated_polynomial_quadrature.reshape(PARALLEL_TOTAL, N_LON, block_width, NDEG).transpose(1, 0, 2, 3)
    wave_blocks = fourier.reshape(N_LON, block_width, PARALLEL_TOTAL, LEV * 2)
    degree_ids = jnp.arange(NDEG, dtype=jnp.int32)

    def one_block(triple):
        basis, coeffs, block = triple
        summed = jnp.einsum("imn,mia->nam", basis.astype(jnp.float32), coeffs.astype(jnp.float32), precision=maximal_magnitude)
        wave_ids = block * block_width + jnp.arange(block_width, dtype=jnp.int32)
        return jnp.where(degree_ids[:, None, None] >= wave_ids[None, None, :], summed, 0.0)

    stacked = lax.map(one_block, (basis_blocks, wave_blocks, jnp.arange(N_LON, dtype=jnp.int32)))
    spectra = stacked.transpose(1, 2, 0, 3).reshape(NDEG, LEV * 2, M)

    wet = water_indicator.astype(jnp.float32)
    picked_air = column_flux.reshape(-1, AIR_PANEL_PLACES)[heat_feeding_panels]
    sea_flux = jnp.einsum("rckio,rcki->rco", heat_transfer_factors.astype(jnp.float32), picked_air, precision=maximal_magnitude).reshape(OROWS, OCOLS)
    warmed = marine_heat.at[0].add(FLUX_RATE * sea_flux * wet)
    padded = jnp.pad(warmed, ((0, 0), (2, 2), (2, 2)))
    wet_pad = jnp.pad(wet, 2)
    ocean_out = diffuse(diffuse(padded, wet_pad), wet_pad[1:-1, 1:-1])
    return spectra, ocean_out
```

```python
import functools
import math

import jax
import jax.numpy as jnp
from jax import lax
from jax.experimental import pallas as pl
from jax.experimental.pallas import tpu as pltpu
from jax.sharding import PartitionSpec as P

TWO_PI = 6.283185307179586
FLUX_RATE = 0.5
KAPPA = 0.2
MESH_ID = pl.DeviceIdType.MESH
LANES = 128
PACK = 21
BLK_PAD = 64
VMEM_LIMIT = 48 * 1024 * 1024


def shifted(index, offset, count):
    return lax.rem(index + offset, count)


def greet(partners):
    barrier = pltpu.get_barrier_semaphore()
    for partner in partners:
        pl.semaphore_signal(barrier, inc=1, device_id=partner, device_id_type=MESH_ID)
    pl.semaphore_wait(barrier, len(partners))


def remote(src, dst, send_sem, recv_sem, partner):
    return pltpu.make_async_remote_copy(
        src_ref=src,
        dst_ref=dst,
        send_sem=send_sem,
        recv_sem=recv_sem,
        device_id=partner,
        device_id_type=MESH_ID,
    )


def landed(ref, sem):
    pltpu.make_async_copy(ref, ref, sem).wait()


def turn(phase, count, inverse):
    rest = phase - jnp.floor(phase * inverse + 0.5) * count
    part = rest * inverse
    square = part * part
    cosine = jnp.zeros_like(part)
    sine = jnp.zeros_like(part)
    for power in range(8, -1, -1):
        sign = -1.0 if power % 2 else 1.0
        cosine = cosine * square + sign * TWO_PI ** (2 * power) / math.factorial(2 * power)
        sine = sine * square - sign * TWO_PI ** (2 * power + 1) / math.factorial(2 * power + 1)
    return cosine, sine * part


def spread_kernel(
    sizes,
    nodes_ref,
    inverse_ref,
    partial_ref,
    heat_ref,
    sea_ref,
    flux_ref,
    e1_ref,
    e2_ref,
    stage,
    part,
    gathered,
    sea0_send,
    sea0_recv,
    flux0_send,
    flux0_recv,
    sea1_send,
    sea1_recv,
    flux1_send,
    flux1_recv,
    sea2_send,
    sea2_recv,
    flux2_send,
    flux2_recv,
):
    grps, lats, lons, lat_count, lon_local, m_local, block_air = sizes
    g, t, y = (lax.axis_index(name) for name in ("grp", "lat", "lon"))
    lon_per, lat_per = lons // grps, lats // grps
    sea_owner, yy = y // lon_per, lax.rem(y, lon_per)
    flux_owner, tt = t // lat_per, lax.rem(t, lat_per)

    def tables(i):
        count = nodes_ref[i].astype(jnp.float32)
        inverse = inverse_ref[i]
        wide = lons * LANES
        lane = lax.broadcasted_iota(jnp.int32, (8, wide), 1)
        row = lax.broadcasted_iota(jnp.int32, (8, wide), 0)
        inner = lane % LANES
        wave = (lane // LANES) * m_local + inner
        start = y * lon_local
        wave_f = wave.astype(jnp.float32)
        row_f = row.astype(jnp.float32)
        base_f = start.astype(jnp.float32)
        high = turn((base_f + 8 * block_air * row_f) * wave_f, count, inverse)
        low = turn((block_air * row_f) * wave_f, count, inverse)
        slot = turn(row_f * wave_f, count, inverse)
        usable = (inner < m_local) & (2.0 * wave_f < count)
        e2_ref[pl.ds(pl.multiple_of(i * 8, 8), 8), :wide] = jnp.where(usable, slot[0], 0.0)
        e2_ref[pl.ds(pl.multiple_of(i * 8, 8), 8), wide:] = jnp.where(usable, slot[1], 0.0)
        for pair in range(BLK_PAD // 16):
            real, imag = [], []
            for b in (2 * pair, 2 * pair + 1):
                hr, hi = high[0][b : b + 1], high[1][b : b + 1]
                real.append(hr * low[0] - hi * low[1])
                imag.append(hr * low[1] + hi * low[0])
            where = pl.ds(pl.multiple_of(i * BLK_PAD + pair * 16, 16), 16)
            e1_ref[where, :wide] = jnp.concatenate(real, axis=0).astype(jnp.bfloat16)
            e1_ref[where, wide:] = jnp.concatenate(imag, axis=0).astype(jnp.bfloat16)

    def some_tables(low, high):
        lax.fori_loop(low, high, lambda i, c: (tables(i), c)[1], 0)

    rows3 = 3 * lat_count
    lane = lax.broadcasted_iota(jnp.int32, (lat_count, LANES), 1)
    span = PACK * block_air
    for c in range(3):
        whole = partial_ref[...]
        moved = whole if c == 0 else pltpu.roll(whole, 3 * LANES - c * span, 1)
        limit = min(span, lon_local - c * span)
        part[c * lat_count : (c + 1) * lat_count, :] = jnp.where(
            lane < limit, moved[:, :LANES], 0.0
        )
    stage[...] = heat_ref[0].astype(jnp.bfloat16)

    greet(
        [{"grp": shifted(g, d, grps)} for d in range(1, grps)]
        + [{"lon": shifted(y, d, lons)} for d in range(1, lons)]
        + [{"lat": shifted(t, d, lats)} for d in range(1, lats)]
    )

    sea0 = remote(stage, sea_ref.at[t, yy], sea0_send, sea0_recv, {"grp": sea_owner})
    flux0 = remote(
        part, gathered.at[g], flux0_send, flux0_recv.at[g], {"grp": flux_owner}
    )

    @pl.when((g == 0) & (sea_owner != 0))
    def _():
        sea0.start()

    @pl.when((g == 0) & (sea_owner == 0))
    def _():
        sea_ref[t, yy] = stage[...]

    @pl.when(g != flux_owner)
    def _():
        flux0.start()

    some_tables(0, 2)

    @pl.when((g == sea_owner) & (sea_owner != 0))
    def _():
        landed(sea_ref.at[t, yy], sea0_recv)

    @pl.when(g == sea_owner)
    def _():
        for d in range(1, lons):
            remote(
                sea_ref.at[t, yy],
                sea_ref.at[t, yy],
                sea1_send.at[d],
                sea1_recv.at[yy],
                {"lon": shifted(y, d, lons)},
            ).start()

    @pl.when(g == flux_owner)
    def _():
        gathered[g] = part[...]
        for d in range(1, grps):
            other = shifted(g, d, grps)
            landed(gathered.at[other], flux0_recv.at[other])
        total = gathered[0]
        for other in range(1, grps):
            total = total + gathered[other]
        flux_ref[y, tt] = jnp.concatenate(
            [total, jnp.zeros((32 - rows3, LANES), jnp.float32)], axis=0
        ).astype(jnp.bfloat16)
        for d in range(1, lats):
            remote(
                flux_ref.at[y, tt],
                flux_ref.at[y, tt],
                flux1_send.at[d],
                flux1_recv.at[tt],
                {"lat": shifted(t, d, lats)},
            ).start()

    some_tables(2, 4)

    for k in range(lon_per):
        @pl.when(g * lon_per + k != y)
        def _():
            landed(sea_ref.at[t, k], sea1_recv.at[k])

    for d in range(1, lats):
        remote(
            sea_ref.at[t],
            sea_ref.at[t],
            sea2_send.at[d],
            sea2_recv.at[t],
            {"lat": shifted(t, d, lats)},
        ).start()

    for k in range(lat_per):
        @pl.when(g * lat_per + k != t)
        def _():
            landed(flux_ref.at[y, k], flux1_recv.at[k])

    for d in range(1, lons):
        remote(
            flux_ref.at[y],
            flux_ref.at[y],
            flux2_send.at[d],
            flux2_recv.at[y],
            {"lon": shifted(y, d, lons)},
        ).start()

    some_tables(4, lat_count)

    for d in range(1, lons):
        other = shifted(y, d, lons)
        landed(flux_ref.at[other], flux2_recv.at[other])
    for d in range(1, lats):
        other = shifted(t, d, lats)
        landed(sea_ref.at[other], sea2_recv.at[other])

    @pl.when((g == 0) & (sea_owner != 0))
    def _():
        landed(stage, sea0_send)

    @pl.when(g != flux_owner)
    def _():
        landed(part, flux0_send)

    @pl.when(g == sea_owner)
    def _():
        for d in range(1, lons):
            landed(sea_ref.at[t, yy], sea1_send.at[d])

    @pl.when(g == flux_owner)
    def _():
        for d in range(1, lats):
            landed(flux_ref.at[y, tt], flux1_send.at[d])

    for d in range(1, lats):
        landed(sea_ref.at[t], sea2_send.at[d])
    for d in range(1, lons):
        landed(flux_ref.at[y], flux2_send.at[d])


def spectral_kernel(
    sizes,
    sens_ref,
    inverse_ref,
    warmth_ref,
    flux_ref,
    aloft_ref,
    mask_ref,
    e1_ref,
    e2_ref,
    quad_ref,
    heat_ref,
    water_ref,
    spec_ref,
    ocean_ref,
    warmth_in,
    flux_in,
    ext,
    waves,
    waves_in,
    spread,
    sums,
    turned,
    turned_in,
    warmth_send,
    warmth_recv,
    flux_send,
    flux_recv,
    halo_send,
    halo_recv,
    waves_send,
    waves_recv,
    turned_send,
    turned_recv,
):
    grps, lats, lons, lat_count, levels, m_local, degrees, olev, rows, cols = sizes
    g, t, y = (lax.axis_index(name) for name in ("grp", "lat", "lon"))
    wide = lons * LANES
    parts = 2 * levels
    n_local = degrees // lats
    north, south = shifted(t, lats - 1, lats), shifted(t, 1, lats)
    west, east = shifted(y, lons - 1, lons), shifted(y, 1, lons)
    mid_rows, mid_cols = slice(8, 8 + rows), slice(LANES, LANES + cols)
    first_rows, last_rows = slice(8, 16), slice(rows, rows + 8)
    low_rows, high_rows = slice(0, 8), slice(8 + rows, 16 + rows)
    low_cols, high_cols = slice(0, LANES), slice(LANES + cols, 2 * LANES + cols)
    halo = [
        ({"lat": south}, last_rows, low_rows, mid_cols),
        ({"lat": north}, first_rows, high_rows, mid_cols),
        ({"lon": east}, mid_rows, mid_rows, low_cols),
        ({"lon": west}, mid_rows, mid_rows, high_cols),
        ({"lat": south, "lon": east}, last_rows, low_rows, low_cols),
        ({"lat": south, "lon": west}, last_rows, low_rows, high_cols),
        ({"lat": north, "lon": east}, first_rows, high_rows, low_cols),
        ({"lat": north, "lon": west}, first_rows, high_rows, high_cols),
    ]

    for level in range(olev):
        ext[level, mid_rows, mid_cols] = heat_ref[level]
    wet_mid = water_ref[...].astype(jnp.float32)
    ext[olev, mid_rows, mid_cols] = wet_mid

    greet(
        [{"grp": shifted(g, d, grps)} for d in range(1, grps)]
        + [{"lon": shifted(y, d, lons)} for d in range(1, lons)]
        + [{"lat": shifted(t, d, lats)} for d in range(1, lats)]
        + [partner for partner, _, _, _ in halo[4:]]
    )

    flux_copy = remote(
        flux_ref, flux_in.at[g], flux_send, flux_recv.at[g], {"grp": jnp.int32(0)}
    )

    @pl.when(g != 0)
    def _():
        flux_copy.start()

    for d in range(1, grps):
        remote(
            warmth_ref,
            warmth_in.at[g],
            warmth_send.at[d],
            warmth_recv.at[g],
            {"grp": shifted(g, d, grps)},
        ).start()

    @pl.when(g == 0)
    def _():
        total = flux_ref[...]
        for other in range(1, grps):
            landed(flux_in.at[other], flux_recv.at[other])
            total = total + flux_in[other]
        ext[0, mid_rows, mid_cols] = heat_ref[0] + FLUX_RATE * total * wet_mid

    for index, (partner, src_rows, dst_rows, dst_cols) in enumerate(halo):
        remote(
            ext.at[:, src_rows, mid_cols],
            ext.at[:, dst_rows, dst_cols],
            halo_send.at[index],
            halo_recv.at[index],
            partner,
        ).start()

    warmth_in[g] = warmth_ref[...]
    for d in range(1, grps):
        other = shifted(g, d, grps)
        landed(warmth_in.at[other], warmth_recv.at[other])
    warmth = warmth_in[0]
    for other in range(1, grps):
        warmth = warmth + warmth_in[other]
    warmth = warmth * mask_ref[...]
    forced = jnp.concatenate(
        [aloft_ref[8 * l : 8 * l + 8, :] + sens_ref[l] * warmth for l in range(levels)], axis=0
    )
    lane = lax.broadcasted_iota(jnp.int32, forced.shape, 1)
    blocks = jnp.concatenate(
        [jnp.where(lane // BLK_PAD == i, forced, 0.0) for i in range(lat_count)], axis=0
    ).astype(jnp.bfloat16)
    real = jnp.dot(blocks, e1_ref[:, :wide], preferred_element_type=jnp.float32)
    imag = jnp.dot(blocks, e1_ref[:, wide:], preferred_element_type=jnp.float32)
    for i in range(lat_count):
        slot_r = e2_ref[8 * i : 8 * i + 8, :wide] * inverse_ref[i]
        slot_i = e2_ref[8 * i : 8 * i + 8, wide:] * inverse_ref[i]
        for l in range(levels):
            at = (i * levels + l) * 8
            re, im = real[at : at + 8], imag[at : at + 8]
            out_r = jnp.sum(re * slot_r - im * slot_i, axis=0, keepdims=True)
            out_i = jnp.sum(re * slot_i + im * slot_r, axis=0, keepdims=True)
            for c, out in enumerate((out_r, out_i)):
                row = (2 * l + c) * lat_count + i
                for k in range(lons):
                    waves[k, row : row + 1, :] = out[:, k * LANES : (k + 1) * LANES]

    for d in range(1, lons):
        other = shifted(y, d, lons)
        remote(
            waves.at[other], waves_in.at[y], waves_send.at[d], waves_recv.at[y], {"lon": other}
        ).start()

    for index, (partner, src_rows, dst_rows, dst_cols) in enumerate(halo):
        landed(ext.at[:, dst_rows, dst_cols], halo_recv.at[index])
    shape = (rows + 16, cols + 2 * LANES)
    row_id = lax.broadcasted_iota(jnp.int32, shape, 0) + (t * rows - 8)
    col_id = lax.broadcasted_iota(jnp.int32, shape, 1) + (y * cols - LANES)
    inside = (row_id >= 0) & (row_id < rows * lats) & (col_id >= 0) & (col_id < cols * lons)
    wet = jnp.where(inside, ext[olev], 0.0)
    moves = ((1, 0), (shape[0] - 1, 0), (1, 1), (shape[1] - 1, 1))
    wet_near = [pltpu.roll(wet, shift, axis) for shift, axis in moves]
    for level in range(olev):
        field = ext[level]
        for _ in range(2):
            total = jnp.zeros_like(field)
            for (shift, axis), near in zip(moves, wet_near):
                total = total + near * (pltpu.roll(field, shift, axis) - field)
            field = field + KAPPA * wet * total
        ocean_ref[level] = field[mid_rows, mid_cols]

    waves_in[y] = waves[y]
    for d in range(1, lons):
        other = shifted(y, d, lons)
        landed(waves_in.at[other], waves_recv.at[other])
    total = waves_in[0]
    for other in range(1, lons):
        total = total + waves_in[other]
    total = total.astype(jnp.bfloat16).astype(jnp.float32)
    rest = jnp.zeros((LANES - parts * lat_count, LANES), jnp.float32)
    columns = jnp.transpose(jnp.concatenate([total, rest], axis=0))
    for j in range(parts * lat_count):
        spread[j] = jnp.broadcast_to(columns[:m_local, j : j + 1], (m_local, LANES))

    sums[...] = jnp.zeros_like(sums)

    def chunk(c, carry):
        lanes = pl.ds(pl.multiple_of(c * LANES, LANES), LANES)

        def some_waves(b, inner):
            own = pl.ds(pl.multiple_of(b * 16, 16), 16)
            acc = [jnp.zeros((16, LANES), jnp.float32) for _ in range(parts)]
            for i in range(lat_count):
                quad = quad_ref[i, own, lanes].astype(jnp.float32)
                for a in range(parts):
                    acc[a] = acc[a] + quad * spread[a * lat_count + i, own, :]
            for a in range(parts):
                sums[pl.ds(pl.multiple_of(a * m_local + b * 16, 16), 16), :] = acc[a]
            return inner

        lax.fori_loop(0, m_local // 16, some_waves, 0)
        turned[pl.ds(pl.multiple_of(c * LANES, LANES), LANES), :] = jnp.transpose(
            sums[...]
        ).astype(jnp.bfloat16)
        return carry

    lax.fori_loop(0, degrees // LANES, chunk, 0)

    def block(k):
        return turned.at[pl.ds(pl.multiple_of(k * n_local, 16), n_local), :]

    for d in range(1, lats):
        other = shifted(t, d, lats)
        remote(
            block(other), turned_in.at[t], turned_send.at[d], turned_recv.at[t], {"lat": other}
        ).start()
    result = turned[pl.ds(pl.multiple_of(t * n_local, 16), n_local), :].astype(jnp.float32)
    for d in range(1, lats):
        other = shifted(t, lats - d, lats)
        landed(turned_in.at[other], turned_recv.at[other])
        result = result + turned_in[other].astype(jnp.float32)
    lane = lax.broadcasted_iota(jnp.int32, result.shape, 1)
    degree = lax.broadcasted_iota(jnp.int32, result.shape, 0) + t * n_local
    spec_ref[...] = jnp.where(degree >= lane % m_local + y * m_local, result, 0.0)

    @pl.when(g != 0)
    def _():
        landed(flux_ref, flux_send)

    for d in range(1, grps):
        landed(warmth_ref, warmth_send.at[d])
    for index, (partner, src_rows, dst_rows, dst_cols) in enumerate(halo):
        landed(ext.at[:, src_rows, mid_cols], halo_send.at[index])
    for d in range(1, lons):
        landed(waves.at[0], waves_send.at[d])
    for d in range(1, lats):
        landed(turned_in.at[0], turned_send.at[d])


def per_device(
    aloft_gridpoint,
    parallel_nodes,
    layer_pressure_share,
    layer_sensitivity,
    associated_polynomial_quadrature,
    marine_heat,
    water_indicator,
    heat_feeding_panels,
    heat_transfer_factors,
    skin_warmth_feeding_panels,
    skin_warmth_mapping_factors,
):
    grps, lats, lons = (lax.axis_size(name) for name in ("grp", "lat", "lon"))
    g, y = lax.axis_index("grp"), lax.axis_index("lon")
    levels, lat_count, lon_local = aloft_gridpoint.shape
    block_air = heat_transfer_factors.shape[3]
    blocks = lon_local // block_air
    olev, rows, cols = marine_heat.shape
    m_local, degrees = associated_polynomial_quadrature.shape[1:]
    lon_per, lat_per = lons // grps, lats // grps
    wide = lons * LANES
    vmem = pl.BlockSpec(memory_space=pltpu.VMEM)
    smem = pl.BlockSpec(memory_space=pltpu.SMEM)
    f32, bf16 = jnp.float32, jnp.bfloat16
    dma, dmas = pltpu.SemaphoreType.DMA, lambda n: pltpu.SemaphoreType.DMA((n,))

    lon_ids = y * lon_local + jnp.arange(lon_local, dtype=jnp.int32)
    live = (lon_ids[None, :] < parallel_nodes[:, None]).astype(f32)
    aloft_state = aloft_gridpoint.astype(f32)
    partial_flux = jnp.sum(layer_pressure_share[:, None, None] * aloft_state, axis=0) * live
    partial_flux = jnp.pad(partial_flux, ((0, 0), (0, 3 * LANES - lon_local)))
    inverse = 1.0 / parallel_nodes.astype(f32)

    def by_slot(field):
        split = field.reshape(field.shape[:-1] + (blocks, block_air))
        split = jnp.moveaxis(split, -1, -3)
        pad = [(0, 0)] * (split.ndim - 3) + [(0, 8 - block_air), (0, 0), (0, BLK_PAD - blocks)]
        padded = jnp.pad(split, pad)
        return padded.reshape(-1, lat_count * BLK_PAD)

    sizes = (grps, lats, lons, lat_count, lon_local, m_local, block_air)
    sea_table, flux_table, e1, e2 = pl.pallas_call(
        functools.partial(spread_kernel, sizes),
        out_shape=(
            jax.ShapeDtypeStruct((lats, lon_per, rows, cols), bf16),
            jax.ShapeDtypeStruct((lons, lat_per, 32, LANES), bf16),
            jax.ShapeDtypeStruct((lat_count * BLK_PAD, 2 * wide), bf16),
            jax.ShapeDtypeStruct((lat_count * 8, 2 * wide), f32),
        ),
        in_specs=[smem, smem, vmem, vmem],
        out_specs=(vmem,) * 4,
        scratch_shapes=[
            pltpu.VMEM((rows, cols), bf16),
            pltpu.VMEM((3 * lat_count, LANES), f32),
            pltpu.VMEM((grps, 3 * lat_count, LANES), f32),
            dma,
            dma,
            dma,
            dmas(grps),
            dmas(lons),
            dmas(lon_per),
            dmas(lats),
            dmas(lat_per),
            dmas(lats),
            dmas(lats),
            dmas(lons),
            dmas(lons),
        ],
        compiler_params=pltpu.CompilerParams(
            collective_id=0, has_side_effects=True, vmem_limit_bytes=VMEM_LIMIT
        ),
    )(parallel_nodes, inverse, partial_flux, marine_heat)

    chosen = skin_warmth_feeding_panels.reshape(-1)
    column, row = chosen % lons, chosen // lons
    local = (row // rows) * (lon_per * rows) + (column % lon_per) * rows + row % rows
    local = jnp.where(column // lon_per == g, local, -1)
    table = sea_table.reshape(-1, cols)
    one_hot = (local[:, None] == jnp.arange(table.shape[0], dtype=jnp.int32)[None, :]).astype(bf16)
    picked = jnp.dot(one_hot, table, preferred_element_type=f32).reshape(
        skin_warmth_feeding_panels.shape + (cols,)
    )
    warmth = jnp.sum(skin_warmth_mapping_factors.astype(f32) * picked[:, :, :, None, :], axis=(2, 4))
    warmth = by_slot(warmth.reshape(lat_count, lon_local))

    chosen = heat_feeding_panels.reshape(-1)
    parallel, slot = chosen // (blocks * lons), chosen % (blocks * lons)
    band, lon, block = parallel // lat_count, slot // blocks, slot % blocks
    local = (
        (lon * lat_per + band % lat_per) * 32 + (block // PACK) * lat_count + parallel % lat_count
    )
    local = jnp.where(band // lat_per == g, local, -1)
    table = flux_table.reshape(-1, LANES)
    one_hot = (local[:, None] == jnp.arange(table.shape[0], dtype=jnp.int32)[None, :]).astype(bf16)
    line = jnp.dot(one_hot, table, preferred_element_type=f32)
    lane = jnp.arange(LANES, dtype=jnp.int32)
    line = jnp.where(lane[None, :] // block_air == (block % PACK)[:, None], line, 0.0)
    fold = (lane[:, None] % block_air == jnp.arange(block_air)[None, :]).astype(bf16)
    air = jnp.dot(line.astype(bf16), fold, preferred_element_type=f32)
    air = air.reshape(heat_feeding_panels.shape + (block_air,))
    flux = jnp.sum(
        heat_transfer_factors.astype(f32) * air[..., None], axis=(2, 3)
    ).reshape(rows, cols)

    sizes = (grps, lats, lons, lat_count, levels, m_local, degrees, olev, rows, cols)
    n_local = degrees // lats
    parts = 2 * levels
    width = -(-parts * m_local // LANES) * LANES
    spec, ocean = pl.pallas_call(
        functools.partial(spectral_kernel, sizes),
        out_shape=(
            jax.ShapeDtypeStruct((n_local, width), f32),
            jax.ShapeDtypeStruct((olev, rows, cols), f32),
        ),
        in_specs=[smem, smem] + [vmem] * 9,
        out_specs=(vmem, vmem),
        scratch_shapes=[
            pltpu.VMEM((grps, 8, lat_count * BLK_PAD), f32),
            pltpu.VMEM((grps, rows, cols), f32),
            pltpu.VMEM((olev + 1, rows + 16, cols + 2 * LANES), f32),
            pltpu.VMEM((lons, parts * lat_count, LANES), f32),
            pltpu.VMEM((lons, parts * lat_count, LANES), f32),
            pltpu.VMEM((parts * lat_count, m_local, LANES), f32),
            pltpu.VMEM((width, LANES), f32),
            pltpu.VMEM((degrees, width), bf16),
            pltpu.VMEM((lats, n_local, width), bf16),
            dmas(grps),
            dmas(grps),
            dma,
            dmas(grps),
            dmas(8),
            dmas(8),
            dmas(lons),
            dmas(lons),
            dmas(lats),
            dmas(lats),
        ],
        compiler_params=pltpu.CompilerParams(
            collective_id=1, has_side_effects=True, vmem_limit_bytes=VMEM_LIMIT
        ),
    )(
        layer_sensitivity,
        inverse,
        warmth,
        flux,
        by_slot(aloft_state * live),
        by_slot(live[None]),
        e1,
        e2,
        associated_polynomial_quadrature,
        marine_heat,
        water_indicator,
    )
    spectra = spec[:, : parts * m_local].reshape(n_local, parts, m_local)
    return (spectra, ocean)


def solution(mesh):
    in_specs = (
        P("grp", "lat", "lon"),
        P("lat"),
        P("grp"),
        P("grp"),
        P("lat", "lon", None),
        P("grp", "lat", "lon"),
        P("lat", "lon"),
        P("lat", "lon", None),
        P("lat", "lon", None, None, None),
        P("lat", "lon", None),
        P("lat", "lon", None, None, None),
    )
    out_specs = (P("lat", "grp", "lon"), P("grp", "lat", "lon"))
    return jax.shard_map(
        per_device, mesh=mesh, in_specs=in_specs, out_specs=out_specs, check_vma=False
    )
```

```python
import functools
import math

import jax
import jax.numpy as jnp
from jax import lax
from jax.experimental import pallas as pl
from jax.experimental.pallas import tpu as pltpu
from jax.sharding import PartitionSpec as P

TWO_PI = 6.283185307179586
FLUX_RATE = 0.5
KAPPA = 0.2
MESH_ID = pl.DeviceIdType.MESH
LANES = 128
BLK_PAD = 64
VMEM_LIMIT = 48 * 1024 * 1024


def shifted(index, offset, count):
    return lax.rem(index + offset, count)


def greet(partners):
    barrier = pltpu.get_barrier_semaphore()
    for partner in partners:
        pl.semaphore_signal(barrier, inc=1, device_id=partner, device_id_type=MESH_ID)
    pl.semaphore_wait(barrier, len(partners))


def remote(src, dst, send_sem, recv_sem, partner):
    return pltpu.make_async_remote_copy(
        src_ref=src,
        dst_ref=dst,
        send_sem=send_sem,
        recv_sem=recv_sem,
        device_id=partner,
        device_id_type=MESH_ID,
    )


def landed(ref, sem):
    pltpu.make_async_copy(ref, ref, sem).wait()


def turn(phase, count, inverse):
    rest = phase - jnp.floor(phase * inverse + 0.5) * count
    part = rest * inverse
    square = part * part
    cosine = jnp.zeros_like(part)
    sine = jnp.zeros_like(part)
    for power in range(8, -1, -1):
        sign = -1.0 if power % 2 else 1.0
        cosine = cosine * square + sign * TWO_PI ** (2 * power) / math.factorial(2 * power)
        sine = sine * square - sign * TWO_PI ** (2 * power + 1) / math.factorial(2 * power + 1)
    return cosine, sine * part


def step_kernel(
    sizes,
    nodes_hbm,
    share_hbm,
    sens_hbm,
    quad_hbm,
    warm_hbm,
    cool_hbm,
    aloft_ref,
    heat_ref,
    water_ref,
    warm_ids_ref,
    cool_ids_ref,
    spec_ref,
    ocean_ref,
    nodes_ref,
    share_ref,
    sens_ref,
    quad_ref,
    warm_ref,
    cool_ref,
    sea_ref,
    flux_ref,
    e1_ref,
    e2_ref,
    stage,
    part,
    gathered,
    warmth_out,
    warmth_in,
    flux_out,
    flux_in,
    ext,
    waves,
    waves_in,
    fourier,
    quad_out,
    quad_in,
    sums,
    local_sems,
    own_sem,
    sea1_send,
    sea1_recv,
    flux0_send,
    flux0_recv,
    flux1_send,
    flux1_recv,
    sea2_send,
    sea2_recv,
    flux2_send,
    flux2_recv,
    warmth_send,
    warmth_recv,
    fluxp_send,
    fluxp_recv,
    halo_send,
    halo_recv,
    waves_send,
    waves_recv,
    fourier_send,
    fourier_recv,
    quad_send,
    quad_recv,
    pass_send,
    pass_recv,
):
    (grps, lats, lons, lat_count, levels, lon_local, block_air, m_local, degrees, olev, rows, cols) = sizes
    g, t, y = (lax.axis_index(name) for name in ("grp", "lat", "lon"))
    f32, bf16, i32 = jnp.float32, jnp.bfloat16, jnp.int32
    wide = lons * LANES
    blocks = lon_local // block_air
    parts = 2 * levels
    n_local = degrees // lats
    line = lat_count * BLK_PAD
    lon_per, lat_per = lons // grps, lats // grps
    sea_owner, yy = y // lon_per, lax.rem(y, lon_per)
    flux_owner, tt = t // lat_per, lax.rem(t, lat_per)
    core = lax.rem(g, 2)
    sibling = {"grp": g + 1 - 2 * core}
    north, south = shifted(t, lats - 1, lats), shifted(t, 1, lats)
    west, east = shifted(y, lons - 1, lons), shifted(y, 1, lons)
    mid_rows, mid_cols = slice(8, 8 + rows), slice(LANES, LANES + cols)
    first_rows, last_rows = slice(8, 16), slice(rows, rows + 8)
    low_rows, high_rows = slice(0, 8), slice(8 + rows, 16 + rows)
    low_cols, high_cols = slice(0, LANES), slice(LANES + cols, 2 * LANES + cols)
    halo = [
        ({"lat": south}, last_rows, low_rows, mid_cols),
        ({"lat": north}, first_rows, high_rows, mid_cols),
        ({"lon": east}, mid_rows, mid_rows, low_cols),
        ({"lon": west}, mid_rows, mid_rows, high_cols),
        ({"lat": south, "lon": east}, last_rows, low_rows, low_cols),
        ({"lat": south, "lon": west}, last_rows, low_rows, high_cols),
        ({"lat": north, "lon": east}, first_rows, high_rows, low_cols),
        ({"lat": north, "lon": west}, first_rows, high_rows, high_cols),
    ]
    pairs = lats // 2
    early = 5 * pairs // 8

    fetches = [
        pltpu.make_async_copy(src, dst, local_sems.at[k])
        for k, (src, dst) in enumerate(
            (
                (nodes_hbm, nodes_ref),
                (share_hbm, share_ref),
                (sens_hbm, sens_ref),
                (quad_hbm, quad_ref),
                (cool_hbm, cool_ref),
                (warm_hbm, warm_ref),
            )
        )
    ]
    for fetch in fetches:
        fetch.start()

    stage[...] = heat_ref[0].astype(bf16)
    for level in range(olev):
        ext[level, mid_rows, mid_cols] = heat_ref[level]
    wet_mid = water_ref[...].astype(f32)
    ext[olev, mid_rows, mid_cols] = wet_mid

    for fetch in fetches[:3]:
        fetch.wait()
    lane = lax.broadcasted_iota(i32, (8, line), 1)
    slot = lax.broadcasted_iota(i32, (8, line), 0)
    block = lane % BLK_PAD
    limit = jnp.zeros((8, line), i32)
    for i in range(lat_count):
        limit = jnp.where(lane // BLK_PAD == i, nodes_ref[i], limit)
    live = (block < blocks) & (slot < block_air)
    live = live & (y * lon_local + block * block_air + slot < limit)
    flux_sum = share_ref[0] * aloft_ref[0:8, :]
    for l in range(1, levels):
        flux_sum = flux_sum + share_ref[l] * aloft_ref[8 * l : 8 * l + 8, :]
    flux_sum = jnp.where(live, flux_sum, 0.0)
    tiles = line // LANES
    for k in range(tiles):
        part[8 * k : 8 * k + 8, :] = flux_sum[:, k * LANES : (k + 1) * LANES]

    greet(
        [{"grp": shifted(g, d, grps)} for d in range(1, grps)]
        + [{"lon": shifted(y, d, lons)} for d in range(1, lons)]
        + [{"lat": shifted(t, d, lats)} for d in range(1, lats)]
        + [
            {"grp": shifted(g, d, grps), "lon": shifted(y, e, lons)}
            for d in range(1, grps)
            for e in range(1, lons)
        ]
        + [partner for partner, _, _, _ in halo[4:]]
    )

    @pl.when(g == 0)
    def _():
        for d in range(1, lons):
            remote(
                stage,
                sea_ref.at[t, yy],
                sea1_send.at[d],
                sea1_recv.at[yy],
                {"grp": sea_owner, "lon": shifted(y, d, lons)},
            ).start()

    @pl.when((g == 0) & (sea_owner != 0))
    def _():
        remote(
            stage, sea_ref.at[t, yy], sea1_send.at[0], sea1_recv.at[yy], {"grp": sea_owner}
        ).start()

    @pl.when((g == 0) & (sea_owner == 0))
    def _():
        sea_ref[t, yy] = stage[...]

    @pl.when(g != flux_owner)
    def _():
        remote(
            part, gathered.at[g], flux0_send, flux0_recv.at[g], {"grp": flux_owner}
        ).start()

    def offset_of(rank):
        half = jnp.where(rank % 2 == 1, (rank + 1) // 2, pairs - rank // 2)
        return 2 * lax.rem(half, pairs) + core

    def pack(rank):
        other = shifted(t, offset_of(rank), lats)
        start = other * n_local
        first = jnp.minimum(start // LANES, degrees // LANES - 2)
        offset = start - first * LANES
        lanes = pl.ds(pl.multiple_of(first * LANES, LANES), 2 * LANES)
        at = lax.broadcasted_iota(i32, (16, 2 * LANES), 1)

        def some_rows(b, carry):
            own = pl.ds(pl.multiple_of(b * 16, 16), 16)
            out = [jnp.zeros((16, LANES), f32) for _ in range(lat_count * n_local // LANES + 1)]
            for i in range(lat_count):
                tile, inner = divmod(i * n_local, LANES)
                window = quad_ref[i, own, lanes].astype(f32)
                window = pltpu.roll(window, lax.rem(inner - offset + 2 * LANES, 2 * LANES), 1)
                window = jnp.where((at >= inner) & (at < inner + n_local), window, 0.0)
                out[tile] = out[tile] + window[:, :LANES]
                if inner + n_local > LANES:
                    out[tile + 1] = out[tile + 1] + window[:, LANES:]
            for k in range(lat_count * n_local // LANES):
                quad_out[rank, own, k * LANES : (k + 1) * LANES] = out[k].astype(bf16)
            return carry

        lax.fori_loop(0, m_local // 16, some_rows, 0)

    def quad_copy(rank):
        return remote(
            quad_out.at[rank],
            quad_in.at[t],
            quad_send.at[rank],
            quad_recv.at[t],
            {"lat": shifted(t, offset_of(rank), lats)},
        )

    own_copy = pltpu.make_async_copy(quad_out.at[0], quad_in.at[t], own_sem)

    def pack_and_send(rank, carry):
        pack(rank)

        @pl.when((rank == 0) & (core == 0))
        def _():
            own_copy.start()

        @pl.when((rank != 0) | (core != 0))
        def _():
            quad_copy(rank).start()

        return carry

    fetches[3].wait()
    lax.fori_loop(0, early, pack_and_send, 0)

    for k in range(lon_per):
        @pl.when((g != 0) | (lon_per * g + k != y))
        def _():
            landed(sea_ref.at[t, k], sea1_recv.at[k])

    for d in range(1, lats):
        remote(
            sea_ref.at[t],
            sea_ref.at[t],
            sea2_send.at[d],
            sea2_recv.at[t],
            {"lat": shifted(t, d, lats)},
        ).start()

    @pl.when(g == flux_owner)
    def _():
        gathered[g] = part[...]
        for d in range(1, grps):
            other = shifted(g, d, grps)
            landed(gathered.at[other], flux0_recv.at[other])
        total = gathered[0]
        for other in range(1, grps):
            total = total + gathered[other]
        flux_ref[y, tt] = total.astype(bf16)
        for d in range(1, lats):
            remote(
                flux_ref.at[y, tt],
                flux_ref.at[y, tt],
                flux1_send.at[d],
                flux1_recv.at[tt],
                {"lat": shifted(t, d, lats)},
            ).start()

    def tables(i, carry):
        count = jnp.full((8, LANES), nodes_ref[i], i32).astype(f32)
        inverse = jnp.concatenate([1.0 / count] * lons, axis=1)
        count = jnp.concatenate([count] * lons, axis=1)
        lane = lax.broadcasted_iota(i32, (8, wide), 1)
        row_f = lax.broadcasted_iota(i32, (8, wide), 0).astype(f32)
        inner = lane % LANES
        wave_f = ((lane // LANES) * m_local + inner).astype(f32)
        base_f = (y * lon_local).astype(f32)
        high = turn((base_f + 8 * block_air * row_f) * wave_f, count, inverse)
        low = turn((block_air * row_f) * wave_f, count, inverse)
        fine = turn(row_f * wave_f, count, inverse)
        usable = (inner < m_local) & (2.0 * wave_f < count)
        own = pl.ds(pl.multiple_of(i * 8, 8), 8)
        e2_ref[own, :wide] = jnp.where(usable, fine[0] * inverse, 0.0)
        e2_ref[own, wide:] = jnp.where(usable, fine[1] * inverse, 0.0)
        for pair in range(BLK_PAD // 16):
            real, imag = [], []
            for b in (2 * pair, 2 * pair + 1):
                hr, hi = high[0][b : b + 1], high[1][b : b + 1]
                real.append(hr * low[0] - hi * low[1])
                imag.append(hr * low[1] + hi * low[0])
            where = pl.ds(pl.multiple_of(i * BLK_PAD + pair * 16, 16), 16)
            e1_ref[where, :wide] = jnp.concatenate(real, axis=0).astype(bf16)
            e1_ref[where, wide:] = jnp.concatenate(imag, axis=0).astype(bf16)
        return carry

    lax.fori_loop(0, lat_count // 2, tables, 0)

    for k in range(lat_per):
        @pl.when(g * lat_per + k != t)
        def _():
            landed(flux_ref.at[y, k], flux1_recv.at[k])

    for d in range(1, lons):
        remote(
            flux_ref.at[y],
            flux_ref.at[y],
            flux2_send.at[d],
            flux2_recv.at[y],
            {"lon": shifted(y, d, lons)},
        ).start()

    lax.fori_loop(lat_count // 2, lat_count, tables, 0)

    for d in range(1, lats):
        other = shifted(t, d, lats)
        landed(sea_ref.at[other], sea2_recv.at[other])

    count_rows = lats * lon_per * rows
    table = sea_ref[...].reshape(count_rows, cols).astype(f32)
    table = jnp.concatenate(
        [jnp.transpose(table[k : k + LANES]) for k in range(0, count_rows, LANES)], axis=1
    ).astype(bf16)
    picks = 2 * blocks
    chosen = warm_ids_ref[...]
    column, row = chosen % lons, chosen // lons
    spot = (row // rows) * (lon_per * rows) + (column % lon_per) * rows + row % rows
    spot = jnp.where((column // lon_per == g) & (chosen >= 0), spot, -1)
    fetches[5].wait()
    table_row = lax.broadcasted_iota(i32, (count_rows, LANES), 0)
    pick_id = lax.broadcasted_iota(i32, (picks, 8, LANES), 0)
    pick_lane = lax.broadcasted_iota(i32, (picks, 8, LANES), 2)
    diagonal = pick_lane == (pick_id % 2) * BLK_PAD + pick_id // 2
    out_lane = lax.broadcasted_iota(i32, (8, LANES), 1)
    fill = jnp.zeros((picks, 8 - block_air, LANES), f32)
    warm_sums = []
    for i in range(lat_count):
        one_hot = jnp.where(table_row == spot[i : i + 1, :], 1.0, 0.0).astype(bf16)
        picked = jnp.dot(table, one_hot, preferred_element_type=f32).astype(bf16)
        factor = warm_ref[picks * i : picks * (i + 1)].astype(f32)
        factor = jnp.concatenate([factor, fill], axis=1).reshape(picks * 8, LANES).astype(bf16)
        product = jnp.dot(factor, picked, preferred_element_type=f32)
        product = product.reshape(picks, 8, LANES)
        total = jnp.sum(jnp.where(diagonal, product, 0.0), axis=0)
        warm_sums.append(total + pltpu.roll(total, BLK_PAD, 1))
    for k in range(tiles):
        warmth_out[:, k * LANES : (k + 1) * LANES] = jnp.where(
            out_lane < BLK_PAD, warm_sums[2 * k], warm_sums[2 * k + 1]
        )
    for d in range(1, grps):
        remote(
            warmth_out,
            warmth_in.at[g],
            warmth_send.at[d],
            warmth_recv.at[g],
            {"grp": shifted(g, d, grps)},
        ).start()

    lax.fori_loop(early, pairs, pack_and_send, 0)

    for d in range(1, lons):
        other = shifted(y, d, lons)
        landed(flux_ref.at[other], flux2_recv.at[other])
    chosen = cool_ids_ref[0:1, :]
    parallel, place = chosen // (blocks * lons), chosen % (blocks * lons)
    band, within = parallel // lat_count, parallel % lat_count
    lon, blk = place // blocks, place % blocks
    group = (lon * lat_per + band % lat_per) * tiles + within // 2
    group = jnp.where(band // lat_per == g, group, -1)
    spot = (within % 2) * BLK_PAD + blk
    group_count = lons * lat_per * tiles
    one_hot = jnp.where(
        lax.broadcasted_iota(i32, (LANES, LANES), 0) == spot, 1.0, 0.0
    ).astype(bf16)
    found = jnp.dot(
        flux_ref[...].reshape(group_count * 8, LANES), one_hot, preferred_element_type=f32
    ).reshape(group_count, 8, LANES)
    group_id = lax.broadcasted_iota(i32, (group_count, 8, LANES), 0)
    air = jnp.sum(jnp.where(group_id == group[None], found, 0.0), axis=0)
    width = LANES * 8
    repeat = jnp.where(
        lax.broadcasted_iota(i32, (LANES, width), 0)
        == lax.broadcasted_iota(i32, (LANES, width), 1) // 8,
        1.0,
        0.0,
    ).astype(bf16)
    air = jnp.dot(air.astype(bf16), repeat, preferred_element_type=f32)
    own_slot = lax.broadcasted_iota(i32, (8, width), 1) % 8 == lax.broadcasted_iota(
        i32, (8, width), 0
    )
    air = jnp.sum(jnp.where(own_slot, air, 0.0), axis=0, keepdims=True)
    per_row = width // rows
    air = jnp.where(
        lax.broadcasted_iota(i32, (rows, width), 1) // per_row
        == lax.broadcasted_iota(i32, (rows, width), 0),
        air,
        0.0,
    ).astype(bf16)
    fetches[4].wait()
    factor = cool_ref[...].astype(f32)
    factor = jnp.concatenate(
        [factor, jnp.zeros((LANES, 8 - block_air, LANES), f32)], axis=1
    ).reshape(width, LANES)
    flux_out[...] = jnp.dot(air, factor.astype(bf16), preferred_element_type=f32)

    @pl.when(g != 0)
    def _():
        remote(
            flux_out, flux_in.at[g], fluxp_send, fluxp_recv.at[g], {"grp": jnp.int32(0)}
        ).start()

    warmth_in[g] = warmth_out[...]
    for d in range(1, grps):
        other = shifted(g, d, grps)
        landed(warmth_in.at[other], warmth_recv.at[other])
    warmth = warmth_in[0]
    for other in range(1, grps):
        warmth = warmth + warmth_in[other]
    forced = jnp.concatenate(
        [
            jnp.where(live, aloft_ref[8 * l : 8 * l + 8, :] + sens_ref[l] * warmth, 0.0)
            for l in range(levels)
        ],
        axis=0,
    )
    lane = lax.broadcasted_iota(i32, forced.shape, 1)
    stacked = jnp.concatenate(
        [jnp.where(lane // BLK_PAD == i, forced, 0.0) for i in range(lat_count)], axis=0
    ).astype(bf16)
    real = jnp.dot(stacked, e1_ref[:, :wide], preferred_element_type=f32)
    imag = jnp.dot(stacked, e1_ref[:, wide:], preferred_element_type=f32)
    for i in range(lat_count):
        slot_r = e2_ref[8 * i : 8 * i + 8, :wide]
        slot_i = e2_ref[8 * i : 8 * i + 8, wide:]
        for l in range(levels):
            at = (i * levels + l) * 8
            re, im = real[at : at + 8], imag[at : at + 8]
            out_r = jnp.sum(re * slot_r - im * slot_i, axis=0, keepdims=True)
            out_i = jnp.sum(re * slot_i + im * slot_r, axis=0, keepdims=True)
            for c, out in enumerate((out_r, out_i)):
                row = (2 * l + c) * lat_count + i
                for k in range(lons):
                    waves[k, row : row + 1, :] = out[:, k * LANES : (k + 1) * LANES]

    for d in range(1, lons):
        other = shifted(y, d, lons)
        remote(
            waves.at[other], waves_in.at[y], waves_send.at[d], waves_recv.at[y], {"lon": other}
        ).start()

    @pl.when(g == 0)
    def _():
        total = flux_out[...]
        for other in range(1, grps):
            landed(flux_in.at[other], fluxp_recv.at[other])
            total = total + flux_in[other]
        ext[0, mid_rows, mid_cols] = heat_ref[0] + FLUX_RATE * total * wet_mid

    for index, (partner, src_rows, dst_rows, dst_cols) in enumerate(halo):
        remote(
            ext.at[:, src_rows, mid_cols],
            ext.at[:, dst_rows, dst_cols],
            halo_send.at[index],
            halo_recv.at[index],
            partner,
        ).start()

    waves_in[y] = waves[y]
    for d in range(1, lons):
        other = shifted(y, d, lons)
        landed(waves_in.at[other], waves_recv.at[other])
    total = waves_in[0]
    for other in range(1, lons):
        total = total + waves_in[other]
    fourier[t] = total.astype(bf16)
    for d in range(1, lats):
        remote(
            fourier.at[t],
            fourier.at[t],
            fourier_send.at[d],
            fourier_recv.at[t],
            {"lat": shifted(t, d, lats)},
        ).start()

    def source(rank):
        return shifted(t, lats - offset_of(rank), lats)

    def pass_on(rank, carry):
        @pl.when((rank == 0) & (core == 0))
        def _():
            own_copy.wait()

        @pl.when((rank != 0) | (core != 0))
        def _():
            landed(quad_in.at[source(rank)], quad_recv.at[source(rank)])

        remote(
            quad_in.at[source(rank)],
            quad_in.at[source(rank)],
            pass_send.at[rank],
            pass_recv.at[source(rank)],
            sibling,
        ).start()
        return carry

    lax.fori_loop(0, pairs, pass_on, 0)

    for index, (partner, src_rows, dst_rows, dst_cols) in enumerate(halo):
        landed(ext.at[:, dst_rows, dst_cols], halo_recv.at[index])
    shape = (rows + 16, cols + 2 * LANES)
    row_id = lax.broadcasted_iota(i32, shape, 0) + (t * rows - 8)
    col_id = lax.broadcasted_iota(i32, shape, 1) + (y * cols - LANES)
    inside = (row_id >= 0) & (row_id < rows * lats) & (col_id >= 0) & (col_id < cols * lons)
    wet = jnp.where(inside, ext[olev], 0.0)
    moves = ((1, 0), (shape[0] - 1, 0), (1, 1), (shape[1] - 1, 1))
    wet_near = [pltpu.roll(wet, shift, axis) for shift, axis in moves]
    for level in range(olev):
        field = ext[level]
        for _ in range(2):
            total = jnp.zeros_like(field)
            for (shift, axis), near in zip(moves, wet_near):
                total = total + near * (pltpu.roll(field, shift, axis) - field)
            field = field + KAPPA * wet * total
        ocean_ref[level] = field[mid_rows, mid_cols]

    for d in range(1, lats):
        other = shifted(t, d, lats)
        landed(fourier.at[other], fourier_recv.at[other])
    coefs = [fourier[k].astype(f32) for k in range(lats)]
    columns = []
    for a in range(parts):
        tall = jnp.concatenate(
            [coef[a * lat_count : (a + 1) * lat_count] for coef in coefs], axis=0
        )
        columns.append(jnp.transpose(tall)[:m_local])
    columns = jnp.concatenate(columns, axis=0)
    span = lat_count * n_local
    repeat = jnp.where(
        lax.broadcasted_iota(i32, (lats * lat_count, span), 0) % lat_count
        == lax.broadcasted_iota(i32, (lats * lat_count, span), 1) // n_local,
        1.0,
        0.0,
    ).astype(bf16)
    lane = lax.broadcasted_iota(i32, columns.shape, 1)
    sums[...] = jnp.zeros_like(sums)

    def add_source(s):
        own = jnp.where(lane // lat_count == s, columns, 0.0).astype(bf16)
        coef = jnp.dot(own, repeat, preferred_element_type=f32)
        quad = quad_in[s].astype(f32)
        for a in range(parts):
            at = slice(a * m_local, (a + 1) * m_local)
            sums[at, :] = sums[at, :] + coef[at] * quad

    def add_direct(rank, carry):
        add_source(source(rank))
        return carry

    def add_passed(rank, carry):
        s = shifted(source(rank), lats - 1 + 2 * core, lats)
        landed(quad_in.at[s], pass_recv.at[s])
        add_source(s)
        return carry

    lax.fori_loop(0, pairs, add_direct, 0)
    lax.fori_loop(0, pairs, add_passed, 0)

    folded = jnp.zeros((parts * m_local, LANES), f32)
    for i in range(lat_count):
        tile, inner = divmod(i * n_local, LANES)
        if inner + n_local > LANES:
            window = sums[:, tile * LANES : (tile + 2) * LANES]
            folded = folded + pltpu.roll(window, 2 * LANES - inner, 1)[:, :LANES]
        else:
            window = sums[:, tile * LANES : (tile + 1) * LANES]
            folded = folded + (pltpu.roll(window, LANES - inner, 1) if inner else window)
    width = spec_ref.shape[1]
    folded = jnp.concatenate(
        [folded, jnp.zeros((width - parts * m_local, LANES), f32)], axis=0
    )
    result = jnp.transpose(folded)[:n_local]
    lane = lax.broadcasted_iota(i32, result.shape, 1)
    degree = lax.broadcasted_iota(i32, result.shape, 0) + t * n_local
    spec_ref[...] = jnp.where(degree >= lane % m_local + y * m_local, result, 0.0)

    @pl.when(g == 0)
    def _():
        for d in range(1, lons):
            landed(stage, sea1_send.at[d])

    @pl.when((g == 0) & (sea_owner != 0))
    def _():
        landed(stage, sea1_send.at[0])

    @pl.when(g != flux_owner)
    def _():
        landed(part, flux0_send)

    @pl.when(g == flux_owner)
    def _():
        for d in range(1, lats):
            landed(flux_ref.at[y, tt], flux1_send.at[d])

    @pl.when(g != 0)
    def _():
        landed(flux_out, fluxp_send)

    for d in range(1, lats):
        landed(sea_ref.at[t], sea2_send.at[d])
        landed(fourier.at[t], fourier_send.at[d])
    for d in range(1, lons):
        landed(flux_ref.at[y], flux2_send.at[d])
        landed(waves.at[0], waves_send.at[d])
    for d in range(1, grps):
        landed(warmth_out, warmth_send.at[d])
    for index, (partner, src_rows, dst_rows, dst_cols) in enumerate(halo):
        landed(ext.at[:, src_rows, mid_cols], halo_send.at[index])

    def sent(rank, carry):
        @pl.when((rank != 0) | (core != 0))
        def _():
            landed(quad_out.at[rank], quad_send.at[rank])

        landed(quad_in.at[0], pass_send.at[rank])
        return carry

    lax.fori_loop(0, pairs, sent, 0)


def per_device(
    aloft_gridpoint,
    parallel_nodes,
    layer_pressure_share,
    layer_sensitivity,
    associated_polynomial_quadrature,
    marine_heat,
    water_indicator,
    heat_feeding_panels,
    heat_transfer_factors,
    skin_warmth_feeding_panels,
    skin_warmth_mapping_factors,
):
    grps, lats, lons = (lax.axis_size(name) for name in ("grp", "lat", "lon"))
    levels, lat_count, lon_local = aloft_gridpoint.shape
    block_air = heat_transfer_factors.shape[3]
    blocks = lon_local // block_air
    olev, rows, cols = marine_heat.shape
    m_local, degrees = associated_polynomial_quadrature.shape[1:]
    lon_per, lat_per = lons // grps, lats // grps
    wide = lons * LANES
    line = lat_count * BLK_PAD
    parts = 2 * levels
    n_local = degrees // lats
    width = -(-parts * m_local // LANES) * LANES
    warm_ways = skin_warmth_feeding_panels.shape[2]
    cool_ways = heat_feeding_panels.shape[2]
    vmem = pl.BlockSpec(memory_space=pltpu.VMEM)
    hbm = pl.BlockSpec(memory_space=pl.ANY)
    f32, bf16 = jnp.float32, jnp.bfloat16
    dma, dmas = pltpu.SemaphoreType.DMA, lambda n: pltpu.SemaphoreType.DMA((n,))

    aloft = aloft_gridpoint.astype(f32).reshape(levels, lat_count, blocks, block_air)
    aloft = jnp.pad(
        aloft.transpose(0, 3, 1, 2),
        ((0, 0), (0, 8 - block_air), (0, 0), (0, BLK_PAD - blocks)),
    ).reshape(levels * 8, line)
    warm_ids = jnp.pad(
        skin_warmth_feeding_panels.transpose(0, 2, 1),
        ((0, 0), (0, 0), (0, BLK_PAD - blocks)),
        constant_values=-1,
    ).reshape(lat_count, warm_ways * BLK_PAD)
    cool_ids = heat_feeding_panels.reshape(1, rows * cool_ways)

    sizes = (
        grps, lats, lons, lat_count, levels, lon_local, block_air, m_local, degrees, olev, rows, cols
    )
    spec, ocean = pl.pallas_call(
        functools.partial(step_kernel, sizes),
        out_shape=(
            jax.ShapeDtypeStruct((n_local, width), f32),
            jax.ShapeDtypeStruct((olev, rows, cols), f32),
        ),
        in_specs=[hbm] * 6 + [vmem] * 5,
        out_specs=(vmem, vmem),
        scratch_shapes=[
            pltpu.SMEM((lat_count,), jnp.int32),
            pltpu.SMEM((levels,), f32),
            pltpu.SMEM((levels,), f32),
            pltpu.VMEM((lat_count, m_local, degrees), bf16),
            pltpu.VMEM((lat_count * blocks * warm_ways, block_air, cols), bf16),
            pltpu.VMEM((rows * cool_ways, block_air, cols), bf16),
            pltpu.VMEM((lats, lon_per, rows, cols), bf16),
            pltpu.VMEM((lons, lat_per, line // 16, LANES), bf16),
            pltpu.VMEM((line, 2 * wide), bf16),
            pltpu.VMEM((lat_count * 8, 2 * wide), f32),
            pltpu.VMEM((rows, cols), bf16),
            pltpu.VMEM((line // 16, LANES), f32),
            pltpu.VMEM((grps, line // 16, LANES), f32),
            pltpu.VMEM((8, line), f32),
            pltpu.VMEM((grps, 8, line), f32),
            pltpu.VMEM((rows, cols), f32),
            pltpu.VMEM((grps, rows, cols), f32),
            pltpu.VMEM((olev + 1, rows + 16, cols + 2 * LANES), f32),
            pltpu.VMEM((lons, parts * lat_count, LANES), f32),
            pltpu.VMEM((lons, parts * lat_count, LANES), f32),
            pltpu.VMEM((lats, parts * lat_count, LANES), bf16),
            pltpu.VMEM((lats // 2, m_local, lat_count * n_local), bf16),
            pltpu.VMEM((lats, m_local, lat_count * n_local), bf16),
            pltpu.VMEM((parts * m_local, lat_count * n_local), f32),
            dmas(6),
            dma,
            dmas(lons),
            dmas(lon_per),
            dma,
            dmas(grps),
            dmas(lats),
            dmas(lat_per),
            dmas(lats),
            dmas(lats),
            dmas(lons),
            dmas(lons),
            dmas(grps),
            dmas(grps),
            dma,
            dmas(grps),
            dmas(8),
            dmas(8),
            dmas(lons),
            dmas(lons),
            dmas(lats),
            dmas(lats),
            dmas(lats // 2),
            dmas(lats),
            dmas(lats // 2),
            dmas(lats),
        ],
        compiler_params=pltpu.CompilerParams(
            collective_id=0, has_side_effects=True, vmem_limit_bytes=VMEM_LIMIT
        ),
    )(
        parallel_nodes,
        layer_pressure_share,
        layer_sensitivity,
        associated_polynomial_quadrature,
        skin_warmth_mapping_factors.reshape(-1, block_air, cols),
        heat_transfer_factors.reshape(-1, block_air, cols),
        aloft,
        marine_heat,
        water_indicator,
        warm_ids,
        cool_ids,
    )
    spectra = spec[:, : parts * m_local].reshape(n_local, parts, m_local)
    return (spectra, ocean)


def solution(mesh):
    in_specs = (
        P("grp", "lat", "lon"),
        P("lat"),
        P("grp"),
        P("grp"),
        P("lat", "lon", None),
        P("grp", "lat", "lon"),
        P("lat", "lon"),
        P("lat", "lon", None),
        P("lat", "lon", None, None, None),
        P("lat", "lon", None),
        P("lat", "lon", None, None, None),
    )
    out_specs = (P("lat", "grp", "lon"), P("grp", "lat", "lon"))
    return jax.shard_map(
        per_device, mesh=mesh, in_specs=in_specs, out_specs=out_specs, check_vma=False
    )
```

```python
import functools
import math

import jax
import jax.numpy as jnp
from jax import lax
from jax.experimental import pallas as pl
from jax.experimental.pallas import tpu as pltpu
from jax.sharding import PartitionSpec as P

TWO_PI = 6.283185307179586
FLUX_RATE = 0.5
KAPPA = 0.2
MESH_ID = pl.DeviceIdType.MESH
LANES = 128
BLK_PAD = 64
VMEM_LIMIT = 48 * 1024 * 1024


def shifted(index, offset, count):
    return lax.rem(index + offset, count)


def greet(partners, sometimes, extra):
    barrier = pltpu.get_barrier_semaphore()
    for partner in partners:
        pl.semaphore_signal(barrier, inc=1, device_id=partner, device_id_type=MESH_ID)
    for needed, partner in sometimes:
        @pl.when(needed)
        def _(partner=partner):
            pl.semaphore_signal(barrier, inc=1, device_id=partner, device_id_type=MESH_ID)

    pl.semaphore_wait(barrier, len(partners) + extra)


def remote(src, dst, send_sem, recv_sem, partner):
    return pltpu.make_async_remote_copy(
        src_ref=src,
        dst_ref=dst,
        send_sem=send_sem,
        recv_sem=recv_sem,
        device_id=partner,
        device_id_type=MESH_ID,
    )


def landed(ref, sem):
    pltpu.make_async_copy(ref, ref, sem).wait()


def turn(phase, count, inverse):
    rest = phase - jnp.floor(phase * inverse + 0.5) * count
    part = rest * inverse
    square = part * part
    cosine = jnp.zeros_like(part)
    sine = jnp.zeros_like(part)
    for power in range(8, -1, -1):
        sign = -1.0 if power % 2 else 1.0
        cosine = cosine * square + sign * TWO_PI ** (2 * power) / math.factorial(2 * power)
        sine = sine * square - sign * TWO_PI ** (2 * power + 1) / math.factorial(2 * power + 1)
    return cosine, sine * part


def step_kernel(
    sizes,
    nodes_hbm,
    share_hbm,
    sens_hbm,
    quad_hbm,
    warm_hbm,
    cool_hbm,
    aloft_raw_ref,
    heat_ref,
    water_ref,
    warm_raw_ref,
    cool_raw_ref,
    spec_ref,
    ocean_ref,
    nodes_ref,
    share_ref,
    sens_ref,
    quad_ref,
    warm_ref,
    cool_ref,
    sea_ref,
    flux_ref,
    e1_ref,
    e2_ref,
    aloft_ref,
    warm_ids_ref,
    cool_ids_ref,
    stage,
    part,
    gathered,
    warmth_out,
    warmth_in,
    flux_out,
    flux_in,
    ext,
    waves,
    waves_out,
    waves_in,
    fourier,
    quad_out,
    quad_in,
    sums,
    local_sems,
    own_sem,
    sea1_send,
    sea1_recv,
    flux0_send,
    flux0_recv,
    flux1_send,
    flux1_recv,
    sea2_send,
    sea2_recv,
    flux2_send,
    flux2_recv,
    warmth_send,
    warmth_recv,
    fluxp_send,
    fluxp_recv,
    halo_send,
    halo_recv,
    waves_send,
    waves_recv,
    fourier_send,
    fourier_recv,
    quad_send,
    quad_recv,
    pass_send,
    pass_recv,
):
    (grps, lats, lons, lat_count, levels, lon_local, block_air, m_local, degrees, olev, rows, cols) = sizes
    g, t, y = (lax.axis_index(name) for name in ("grp", "lat", "lon"))
    f32, bf16, i32 = jnp.float32, jnp.bfloat16, jnp.int32
    wide = lons * LANES
    blocks = lon_local // block_air
    parts = 2 * levels
    n_local = degrees // lats
    line = lat_count * BLK_PAD
    lon_per, lat_per = lons // grps, lats // grps
    flux_owner, yy = y // lon_per, lax.rem(y, lon_per)
    sea_owner, tt = t // lat_per, lax.rem(t, lat_per)
    core = lax.rem(g, 2)
    sibling = {"grp": g + 1 - 2 * core}
    north, south = shifted(t, lats - 1, lats), shifted(t, 1, lats)
    west, east = shifted(y, lons - 1, lons), shifted(y, 1, lons)
    mid_rows, mid_cols = slice(8, 8 + rows), slice(LANES, LANES + cols)
    first_rows, last_rows = slice(8, 16), slice(rows, rows + 8)
    low_rows, high_rows = slice(0, 8), slice(8 + rows, 16 + rows)
    low_cols, high_cols = slice(0, LANES), slice(LANES + cols, 2 * LANES + cols)
    halo = [
        ({"lat": south}, last_rows, low_rows, mid_cols),
        ({"lat": north}, first_rows, high_rows, mid_cols),
        ({"lon": east}, mid_rows, mid_rows, low_cols),
        ({"lon": west}, mid_rows, mid_rows, high_cols),
        ({"lat": south, "lon": east}, last_rows, low_rows, low_cols),
        ({"lat": south, "lon": west}, last_rows, low_rows, high_cols),
        ({"lat": north, "lon": east}, first_rows, high_rows, low_cols),
        ({"lat": north, "lon": west}, first_rows, high_rows, high_cols),
    ]
    pairs = lats // 2

    fetches = [
        pltpu.make_async_copy(src, dst, local_sems.at[k])
        for k, (src, dst) in enumerate(
            (
                (nodes_hbm, nodes_ref),
                (share_hbm, share_ref),
                (sens_hbm, sens_ref),
                (quad_hbm, quad_ref),
                (cool_hbm, cool_ref),
                (warm_hbm, warm_ref),
            )
        )
    ]
    for fetch in fetches:
        fetch.start()

    stage[...] = heat_ref[0].astype(bf16)
    expected = jnp.where(g == 0, jnp.where(sea_owner == 0, lats - 1, lats), 0)
    keepers = [(g * lat_per + k, {"grp": jnp.int32(0), "lat": g * lat_per + k}) for k in range(lat_per)]
    greet(
        [{"grp": shifted(g, d, grps)} for d in range(1, grps)]
        + [{"lon": shifted(y, d, lons)} for d in range(1, lons)]
        + [{"lat": shifted(t, d, lats)} for d in range(1, lats)]
        + [partner for partner, _, _, _ in halo[4:]],
        [((g != 0) | (at != t), partner) for at, partner in keepers],
        expected,
    )

    @pl.when(g == 0)
    def _():
        for d in range(1, lats):
            remote(
                stage,
                sea_ref.at[y, tt],
                sea1_send.at[d],
                sea1_recv.at[tt],
                {"grp": sea_owner, "lat": shifted(t, d, lats)},
            ).start()

    @pl.when((g == 0) & (sea_owner != 0))
    def _():
        remote(
            stage, sea_ref.at[y, tt], sea1_send.at[0], sea1_recv.at[tt], {"grp": sea_owner}
        ).start()

    @pl.when((g == 0) & (sea_owner == 0))
    def _():
        sea_ref[y, tt] = stage[...]

    def offset_of(rank):
        half = jnp.where(rank % 2 == 1, (rank + 1) // 2, pairs - rank // 2)
        return 2 * lax.rem(half, pairs) + core

    def pack(rank):
        other = shifted(t, offset_of(rank), lats)
        start = other * n_local
        first = jnp.minimum(start // LANES, degrees // LANES - 2)
        offset = start - first * LANES
        lanes = pl.ds(pl.multiple_of(first * LANES, LANES), 2 * LANES)
        at = lax.broadcasted_iota(i32, (16, 2 * LANES), 1)

        def some_rows(b, carry):
            own = pl.ds(pl.multiple_of(b * 16, 16), 16)
            out = [jnp.zeros((16, LANES), f32) for _ in range(lat_count * n_local // LANES + 1)]
            for i in range(lat_count):
                tile, inner = divmod(i * n_local, LANES)
                window = quad_ref[i, own, lanes].astype(f32)
                window = pltpu.roll(window, lax.rem(inner - offset + 2 * LANES, 2 * LANES), 1)
                window = jnp.where((at >= inner) & (at < inner + n_local), window, 0.0)
                out[tile] = out[tile] + window[:, :LANES]
                if inner + n_local > LANES:
                    out[tile + 1] = out[tile + 1] + window[:, LANES:]
            for k in range(lat_count * n_local // LANES):
                quad_out[rank, own, k * LANES : (k + 1) * LANES] = out[k].astype(bf16)
            return carry

        lax.fori_loop(0, m_local // 16, some_rows, 0)

    def quad_copy(rank):
        return remote(
            quad_out.at[rank],
            quad_in.at[t],
            quad_send.at[rank],
            quad_recv.at[t],
            {"lat": shifted(t, offset_of(rank), lats)},
        )

    own_copy = pltpu.make_async_copy(quad_out.at[0], quad_in.at[t], own_sem)

    def pack_and_send(rank, carry):
        pack(rank)

        @pl.when((rank == 0) & (core == 0))
        def _():
            own_copy.start()

        @pl.when((rank != 0) | (core != 0))
        def _():
            quad_copy(rank).start()

        return carry

    def source(rank):
        return shifted(t, lats - offset_of(rank), lats)

    def pass_on(rank, carry):
        @pl.when((rank == 0) & (core == 0))
        def _():
            own_copy.wait()

        @pl.when((rank != 0) | (core != 0))
        def _():
            landed(quad_in.at[source(rank)], quad_recv.at[source(rank)])

        remote(
            quad_in.at[source(rank)],
            quad_in.at[source(rank)],
            pass_send.at[rank],
            pass_recv.at[source(rank)],
            sibling,
        ).start()
        return carry

    fetches[3].wait()
    lax.fori_loop(0, pairs, pack_and_send, 0)

    for fetch in fetches[:3]:
        fetch.wait()
    tiles = line // LANES
    raw = jnp.concatenate([aloft_raw_ref[l].astype(f32) for l in range(levels)], axis=0)
    source_id = lax.broadcasted_iota(i32, (lon_local, 8 * BLK_PAD), 0)
    target_id = lax.broadcasted_iota(i32, (lon_local, 8 * BLK_PAD), 1)
    target_block, target_slot = target_id % BLK_PAD, target_id // BLK_PAD
    sorting = jnp.where(
        (target_block < blocks)
        & (target_slot < block_air)
        & (source_id == target_block * block_air + target_slot),
        1.0,
        0.0,
    ).astype(bf16)
    by_slot = jnp.dot(raw.astype(bf16), sorting, preferred_element_type=f32)
    aloft_ref[...] = jnp.zeros_like(aloft_ref)
    out_lane = lax.broadcasted_iota(i32, (8, LANES), 1)
    out_row = lax.broadcasted_iota(i32, (8, LANES), 0)
    for l in range(levels):
        for q in range(block_air):
            k = q // 2
            two = by_slot[8 * l : 8 * l + 8, k * LANES : (k + 1) * LANES]
            other = pltpu.roll(two, BLK_PAD, 1)
            both = jnp.where((out_lane < BLK_PAD) == (q % 2 == 0), two, other)
            for k in range(tiles):
                mine = out_row == 2 * k + out_lane // BLK_PAD
                aloft_ref[8 * l + q : 8 * l + q + 1, k * LANES : (k + 1) * LANES] = jnp.sum(
                    jnp.where(mine, both, 0.0), axis=0, keepdims=True
                )
    lane = lax.broadcasted_iota(i32, (8, line), 1)
    slot = lax.broadcasted_iota(i32, (8, line), 0)
    block = lane % BLK_PAD
    limit = jnp.zeros((8, line), i32)
    for i in range(lat_count):
        limit = jnp.where(lane // BLK_PAD == i, nodes_ref[i], limit)
    live = (block < blocks) & (slot < block_air)
    live = live & (y * lon_local + block * block_air + slot < limit)
    flux_sum = share_ref[0] * aloft_ref[0:8, :]
    for l in range(1, levels):
        flux_sum = flux_sum + share_ref[l] * aloft_ref[8 * l : 8 * l + 8, :]
    flux_sum = jnp.where(live, flux_sum, 0.0)
    for k in range(tiles):
        part[8 * k : 8 * k + 8, :] = flux_sum[:, k * LANES : (k + 1) * LANES]

    @pl.when(g != flux_owner)
    def _():
        remote(
            part, gathered.at[g], flux0_send, flux0_recv.at[g], {"grp": flux_owner}
        ).start()

    for k in range(lat_per):
        @pl.when((g != 0) | (lat_per * g + k != t))
        def _():
            landed(sea_ref.at[y, k], sea1_recv.at[k])

    for d in range(1, lons):
        remote(
            sea_ref.at[y],
            sea_ref.at[y],
            sea2_send.at[d],
            sea2_recv.at[y],
            {"lon": shifted(y, d, lons)},
        ).start()

    for level in range(olev):
        ext[level, mid_rows, mid_cols] = heat_ref[level]
    wet_mid = water_ref[...].astype(f32)
    ext[olev, mid_rows, mid_cols] = wet_mid

    def tables(i, carry):
        count = jnp.full((8, LANES), nodes_ref[i], i32).astype(f32)
        inverse = jnp.concatenate([1.0 / count] * lons, axis=1)
        count = jnp.concatenate([count] * lons, axis=1)
        lane = lax.broadcasted_iota(i32, (8, wide), 1)
        row_f = lax.broadcasted_iota(i32, (8, wide), 0).astype(f32)
        inner = lane % LANES
        wave_f = ((lane // LANES) * m_local + inner).astype(f32)
        base_f = (y * lon_local).astype(f32)
        high = turn((base_f + 8 * block_air * row_f) * wave_f, count, inverse)
        low = turn((block_air * row_f) * wave_f, count, inverse)
        fine = turn(row_f * wave_f, count, inverse)
        usable = (inner < m_local) & (2.0 * wave_f < count)
        own = pl.ds(pl.multiple_of(i * 8, 8), 8)
        e2_ref[own, :wide] = jnp.where(usable, fine[0] * inverse, 0.0)
        e2_ref[own, wide:] = jnp.where(usable, fine[1] * inverse, 0.0)
        for pair in range(BLK_PAD // 16):
            real, imag = [], []
            for b in (2 * pair, 2 * pair + 1):
                hr, hi = high[0][b : b + 1], high[1][b : b + 1]
                real.append(hr * low[0] - hi * low[1])
                imag.append(hr * low[1] + hi * low[0])
            where = pl.ds(pl.multiple_of(i * BLK_PAD + pair * 16, 16), 16)
            e1_ref[where, :wide] = jnp.concatenate(real, axis=0).astype(bf16)
            e1_ref[where, wide:] = jnp.concatenate(imag, axis=0).astype(bf16)
        return carry

    lax.fori_loop(0, lat_count // 2, tables, 0)

    @pl.when(g == flux_owner)
    def _():
        gathered[g] = part[...]
        for d in range(1, grps):
            other = shifted(g, d, grps)
            landed(gathered.at[other], flux0_recv.at[other])
        total = gathered[0]
        for other in range(1, grps):
            total = total + gathered[other]
        flux_ref[t, yy] = total.astype(bf16)
        for d in range(1, lons):
            remote(
                flux_ref.at[t, yy],
                flux_ref.at[t, yy],
                flux1_send.at[d],
                flux1_recv.at[yy],
                {"lon": shifted(y, d, lons)},
            ).start()

    lax.fori_loop(lat_count // 2, lat_count, tables, 0)

    for k in range(lon_per):
        @pl.when(g * lon_per + k != y)
        def _():
            landed(flux_ref.at[t, k], flux1_recv.at[k])

    for d in range(1, lats):
        remote(
            flux_ref.at[t],
            flux_ref.at[t],
            flux2_send.at[d],
            flux2_recv.at[t],
            {"lat": shifted(t, d, lats)},
        ).start()

    for d in range(1, lons):
        other = shifted(y, d, lons)
        landed(sea_ref.at[other], sea2_recv.at[other])

    count_rows = lons * lat_per * rows
    table = sea_ref[...].reshape(count_rows, cols).astype(f32)
    table = jnp.concatenate(
        [jnp.transpose(table[k : k + LANES]) for k in range(0, count_rows, LANES)], axis=1
    ).astype(bf16)
    picks = 2 * blocks
    warm_ids_ref[...] = jnp.full_like(warm_ids_ref, -1)
    for i in range(lat_count):
        for k in range(warm_raw_ref.shape[1]):
            warm_ids_ref[i : i + 1, k * BLK_PAD : k * BLK_PAD + blocks] = warm_raw_ref[
                i, k : k + 1, :
            ]
    chosen = warm_ids_ref[...]
    column, row = chosen % lons, chosen // lons
    band = row // rows
    spot = (column * lat_per + band % lat_per) * rows + row % rows
    spot = jnp.where((band // lat_per == g) & (chosen >= 0), spot, -1)
    fetches[5].wait()
    table_row = lax.broadcasted_iota(i32, (count_rows, LANES), 0)
    pick_id = lax.broadcasted_iota(i32, (picks, 8, LANES), 0)
    pick_lane = lax.broadcasted_iota(i32, (picks, 8, LANES), 2)
    diagonal = pick_lane == (pick_id % 2) * BLK_PAD + pick_id // 2
    fill = jnp.zeros((picks, 8 - block_air, LANES), f32)
    warm_sums = []
    for i in range(lat_count):
        one_hot = jnp.where(table_row == spot[i : i + 1, :], 1.0, 0.0).astype(bf16)
        picked = jnp.dot(table, one_hot, preferred_element_type=f32).astype(bf16)
        factor = warm_ref[picks * i : picks * (i + 1)].astype(f32)
        factor = jnp.concatenate([factor, fill], axis=1).reshape(picks * 8, LANES).astype(bf16)
        product = jnp.dot(factor, picked, preferred_element_type=f32)
        product = product.reshape(picks, 8, LANES)
        total = jnp.sum(jnp.where(diagonal, product, 0.0), axis=0)
        warm_sums.append(total + pltpu.roll(total, BLK_PAD, 1))
    for k in range(tiles):
        warmth_out[:, k * LANES : (k + 1) * LANES] = jnp.where(
            out_lane < BLK_PAD, warm_sums[2 * k], warm_sums[2 * k + 1]
        )
    for d in range(1, grps):
        remote(
            warmth_out,
            warmth_in.at[g],
            warmth_send.at[d],
            warmth_recv.at[g],
            {"grp": shifted(g, d, grps)},
        ).start()

    warmth_in[g] = warmth_out[...]
    for d in range(1, grps):
        other = shifted(g, d, grps)
        landed(warmth_in.at[other], warmth_recv.at[other])
    warmth = warmth_in[0]
    for other in range(1, grps):
        warmth = warmth + warmth_in[other]
    forced = jnp.concatenate(
        [
            jnp.where(live, aloft_ref[8 * l : 8 * l + 8, :] + sens_ref[l] * warmth, 0.0)
            for l in range(levels)
        ],
        axis=0,
    )
    lane = lax.broadcasted_iota(i32, forced.shape, 1)
    stacked = jnp.concatenate(
        [jnp.where(lane // BLK_PAD == i, forced, 0.0) for i in range(lat_count)], axis=0
    ).astype(bf16)
    real = jnp.dot(stacked, e1_ref[:, :wide], preferred_element_type=f32)
    imag = jnp.dot(stacked, e1_ref[:, wide:], preferred_element_type=f32)
    for i in range(lat_count):
        slot_r = e2_ref[8 * i : 8 * i + 8, :wide]
        slot_i = e2_ref[8 * i : 8 * i + 8, wide:]
        for l in range(levels):
            at = (i * levels + l) * 8
            re, im = real[at : at + 8], imag[at : at + 8]
            out_r = jnp.sum(re * slot_r - im * slot_i, axis=0, keepdims=True)
            out_i = jnp.sum(re * slot_i + im * slot_r, axis=0, keepdims=True)
            for c, out in enumerate((out_r, out_i)):
                row = (2 * l + c) * lat_count + i
                for k in range(lons):
                    waves[k, row : row + 1, :] = out[:, k * LANES : (k + 1) * LANES]

    waves_out[...] = waves[...].astype(bf16)
    for d in range(1, lons):
        other = shifted(y, d, lons)
        remote(
            waves_out.at[other],
            waves_in.at[y],
            waves_send.at[d],
            waves_recv.at[y],
            {"lon": other},
        ).start()

    for d in range(1, lats):
        other = shifted(t, d, lats)
        landed(flux_ref.at[other], flux2_recv.at[other])
    ways = cool_raw_ref.shape[0]
    for k in range(ways):
        cool_ids_ref[0:1, k * rows : (k + 1) * rows] = cool_raw_ref[k : k + 1, :]
    chosen = cool_ids_ref[0:1, :]
    parallel, place = chosen // (blocks * lons), chosen % (blocks * lons)
    band, within = parallel // lat_count, parallel % lat_count
    lon, blk = place // blocks, place % blocks
    group = (band * lon_per + lon % lon_per) * tiles + within // 2
    group = jnp.where(lon // lon_per == g, group, -1)
    spot = (within % 2) * BLK_PAD + blk
    group_count = lats * lon_per * tiles
    one_hot = jnp.where(
        lax.broadcasted_iota(i32, (LANES, LANES), 0) == spot, 1.0, 0.0
    ).astype(bf16)
    found = jnp.dot(
        flux_ref[...].reshape(group_count * 8, LANES), one_hot, preferred_element_type=f32
    ).reshape(group_count, 8, LANES)
    group_id = lax.broadcasted_iota(i32, (group_count, 8, LANES), 0)
    air = jnp.sum(jnp.where(group_id == group[None], found, 0.0), axis=0)
    width = rows * block_air * 8
    to = lax.broadcasted_iota(i32, (LANES, width), 1)
    repeat = jnp.where(
        (to % 8 < ways)
        & (lax.broadcasted_iota(i32, (LANES, width), 0) == (to % 8) * rows + to // (8 * block_air)),
        1.0,
        0.0,
    ).astype(bf16)
    air = jnp.dot(air.astype(bf16), repeat, preferred_element_type=f32)
    to = lax.broadcasted_iota(i32, (8, width), 1)
    own_slot = (to // 8) % block_air == lax.broadcasted_iota(i32, (8, width), 0)
    air = jnp.sum(jnp.where(own_slot, air, 0.0), axis=0, keepdims=True)
    air = jnp.where(
        lax.broadcasted_iota(i32, (rows, width), 1) // (8 * block_air)
        == lax.broadcasted_iota(i32, (rows, width), 0),
        air,
        0.0,
    ).astype(bf16)
    fetches[4].wait()
    factor = cool_ref[...].astype(f32)
    factor = jnp.concatenate(
        [factor, jnp.zeros((rows * block_air, 8 - ways, LANES), f32)], axis=1
    ).reshape(width, LANES)
    flux_out[...] = jnp.dot(air, factor.astype(bf16), preferred_element_type=f32)

    @pl.when(g != 0)
    def _():
        remote(
            flux_out, flux_in.at[g], fluxp_send, fluxp_recv.at[g], {"grp": jnp.int32(0)}
        ).start()

    lax.fori_loop(0, pairs // 2, pass_on, 0)

    total = waves[y]
    for d in range(1, lons):
        other = shifted(y, d, lons)
        landed(waves_in.at[other], waves_recv.at[other])
        total = total + waves_in[other].astype(f32)
    fourier[t] = total.astype(bf16)

    def send_fourier(offset):
        @pl.when(offset != 0)
        def _():
            remote(
                fourier.at[t],
                fourier.at[t],
                fourier_send.at[offset],
                fourier_recv.at[t],
                {"lat": shifted(t, offset, lats)},
            ).start()

    def send_near(rank, carry):
        send_fourier(offset_of(rank))
        return carry

    def send_far(rank, carry):
        send_fourier(offset_of(rank) + 1 - 2 * core)
        return carry

    lax.fori_loop(0, pairs, send_near, 0)
    lax.fori_loop(0, pairs, send_far, 0)

    @pl.when(g == 0)
    def _():
        total = flux_out[...]
        for other in range(1, grps):
            landed(flux_in.at[other], fluxp_recv.at[other])
            total = total + flux_in[other]
        ext[0, mid_rows, mid_cols] = heat_ref[0] + FLUX_RATE * total * wet_mid

    for index, (partner, src_rows, dst_rows, dst_cols) in enumerate(halo):
        remote(
            ext.at[:, src_rows, mid_cols],
            ext.at[:, dst_rows, dst_cols],
            halo_send.at[index],
            halo_recv.at[index],
            partner,
        ).start()

    lax.fori_loop(pairs // 2, pairs, pass_on, 0)

    span = lat_count * n_local
    repeat_row = lax.broadcasted_iota(i32, (LANES, span), 0)
    repeat = jnp.where(
        (repeat_row < parts * lat_count)
        & (repeat_row % lat_count == lax.broadcasted_iota(i32, (LANES, span), 1) // n_local),
        1.0,
        0.0,
    ).astype(bf16)
    fill = jnp.zeros((LANES - parts * lat_count, LANES), f32)
    part_lane = lax.broadcasted_iota(i32, (m_local, LANES), 1) // lat_count
    sums[...] = jnp.zeros_like(sums)

    def add_source(s):
        @pl.when(s != t)
        def _():
            landed(fourier.at[s], fourier_recv.at[s])

        columns = jnp.transpose(jnp.concatenate([fourier[s].astype(f32), fill], axis=0))[:m_local]
        own = jnp.concatenate(
            [jnp.where(part_lane == a, columns, 0.0) for a in range(parts)], axis=0
        ).astype(bf16)
        coef = jnp.dot(own, repeat, preferred_element_type=f32)
        quad = quad_in[s].astype(f32)
        for a in range(parts):
            at = slice(a * m_local, (a + 1) * m_local)
            sums[at, :] = sums[at, :] + coef[at] * quad

    def add_direct(rank, carry):
        add_source(source(rank))
        return carry

    def add_passed(rank, carry):
        s = shifted(source(rank), lats - 1 + 2 * core, lats)
        landed(quad_in.at[s], pass_recv.at[s])
        add_source(s)
        return carry

    lax.fori_loop(0, pairs, add_direct, 0)

    for index, (partner, src_rows, dst_rows, dst_cols) in enumerate(halo):
        landed(ext.at[:, dst_rows, dst_cols], halo_recv.at[index])
    shape = (rows + 16, cols + 2 * LANES)
    row_id = lax.broadcasted_iota(i32, shape, 0) + (t * rows - 8)
    col_id = lax.broadcasted_iota(i32, shape, 1) + (y * cols - LANES)
    inside = (row_id >= 0) & (row_id < rows * lats) & (col_id >= 0) & (col_id < cols * lons)
    wet = jnp.where(inside, ext[olev], 0.0)
    moves = ((1, 0), (shape[0] - 1, 0), (1, 1), (shape[1] - 1, 1))
    wet_near = [pltpu.roll(wet, shift, axis) for shift, axis in moves]
    for level in range(olev):
        field = ext[level]
        for _ in range(2):
            total = jnp.zeros_like(field)
            for (shift, axis), near in zip(moves, wet_near):
                total = total + near * (pltpu.roll(field, shift, axis) - field)
            field = field + KAPPA * wet * total
        ocean_ref[level] = field[mid_rows, mid_cols]

    lax.fori_loop(0, pairs, add_passed, 0)

    folded = jnp.zeros((parts * m_local, LANES), f32)
    for i in range(lat_count):
        tile, inner = divmod(i * n_local, LANES)
        if inner + n_local > LANES:
            window = sums[:, tile * LANES : (tile + 2) * LANES]
            folded = folded + pltpu.roll(window, 2 * LANES - inner, 1)[:, :LANES]
        else:
            window = sums[:, tile * LANES : (tile + 1) * LANES]
            folded = folded + (pltpu.roll(window, LANES - inner, 1) if inner else window)
    width = spec_ref.shape[1]
    folded = jnp.concatenate(
        [folded, jnp.zeros((width - parts * m_local, LANES), f32)], axis=0
    )
    result = jnp.transpose(folded)[:n_local]
    lane = lax.broadcasted_iota(i32, result.shape, 1)
    degree = lax.broadcasted_iota(i32, result.shape, 0) + t * n_local
    spec_ref[...] = jnp.where(degree >= lane % m_local + y * m_local, result, 0.0)

    @pl.when(g == 0)
    def _():
        for d in range(1, lats):
            landed(stage, sea1_send.at[d])

    @pl.when((g == 0) & (sea_owner != 0))
    def _():
        landed(stage, sea1_send.at[0])

    @pl.when(g != flux_owner)
    def _():
        landed(part, flux0_send)

    @pl.when(g == flux_owner)
    def _():
        for d in range(1, lons):
            landed(flux_ref.at[t, yy], flux1_send.at[d])

    @pl.when(g != 0)
    def _():
        landed(flux_out, fluxp_send)

    for d in range(1, lats):
        landed(flux_ref.at[t], flux2_send.at[d])
        landed(fourier.at[t], fourier_send.at[d])
    for d in range(1, lons):
        landed(sea_ref.at[y], sea2_send.at[d])
        landed(waves_out.at[0], waves_send.at[d])
    for d in range(1, grps):
        landed(warmth_out, warmth_send.at[d])
    for index, (partner, src_rows, dst_rows, dst_cols) in enumerate(halo):
        landed(ext.at[:, src_rows, mid_cols], halo_send.at[index])

    def sent(rank, carry):
        @pl.when((rank != 0) | (core != 0))
        def _():
            landed(quad_out.at[rank], quad_send.at[rank])

        landed(quad_in.at[0], pass_send.at[rank])
        return carry

    lax.fori_loop(0, pairs, sent, 0)


def per_device(
    aloft_gridpoint,
    parallel_nodes,
    layer_pressure_share,
    layer_sensitivity,
    associated_polynomial_quadrature,
    marine_heat,
    water_indicator,
    heat_feeding_panels,
    heat_transfer_factors,
    skin_warmth_feeding_panels,
    skin_warmth_mapping_factors,
):
    grps, lats, lons = (lax.axis_size(name) for name in ("grp", "lat", "lon"))
    levels, lat_count, lon_local = aloft_gridpoint.shape
    block_air = heat_transfer_factors.shape[3]
    blocks = lon_local // block_air
    olev, rows, cols = marine_heat.shape
    m_local, degrees = associated_polynomial_quadrature.shape[1:]
    lon_per, lat_per = lons // grps, lats // grps
    wide = lons * LANES
    line = lat_count * BLK_PAD
    parts = 2 * levels
    n_local = degrees // lats
    width = -(-parts * m_local // LANES) * LANES
    warm_ways = skin_warmth_feeding_panels.shape[2]
    cool_ways = heat_feeding_panels.shape[2]
    vmem = pl.BlockSpec(memory_space=pltpu.VMEM)
    hbm = pl.BlockSpec(memory_space=pl.ANY)
    f32, bf16 = jnp.float32, jnp.bfloat16
    dma, dmas = pltpu.SemaphoreType.DMA, lambda n: pltpu.SemaphoreType.DMA((n,))

    warm_ids = skin_warmth_feeding_panels.transpose(0, 2, 1)
    cool_ids = heat_feeding_panels[:, 0, :].transpose(1, 0)
    cool_factors = heat_transfer_factors.transpose(0, 1, 3, 2, 4)

    sizes = (
        grps, lats, lons, lat_count, levels, lon_local, block_air, m_local, degrees, olev, rows, cols
    )
    spec, ocean = pl.pallas_call(
        functools.partial(step_kernel, sizes),
        out_shape=(
            jax.ShapeDtypeStruct((n_local, width), f32),
            jax.ShapeDtypeStruct((olev, rows, cols), f32),
        ),
        in_specs=[hbm] * 6 + [vmem] * 5,
        out_specs=(vmem, vmem),
        scratch_shapes=[
            pltpu.SMEM((lat_count,), jnp.int32),
            pltpu.SMEM((levels,), f32),
            pltpu.SMEM((levels,), f32),
            pltpu.VMEM((lat_count, m_local, degrees), bf16),
            pltpu.VMEM((lat_count * blocks * warm_ways, block_air, cols), bf16),
            pltpu.VMEM((rows * block_air, cool_ways, cols), bf16),
            pltpu.VMEM((lons, lat_per, rows, cols), bf16),
            pltpu.VMEM((lats, lon_per, line // 16, LANES), bf16),
            pltpu.VMEM((line, 2 * wide), bf16),
            pltpu.VMEM((lat_count * 8, 2 * wide), f32),
            pltpu.VMEM((levels * 8, line), f32),
            pltpu.VMEM((lat_count, warm_ways * BLK_PAD), jnp.int32),
            pltpu.VMEM((8, rows * cool_ways), jnp.int32),
            pltpu.VMEM((rows, cols), bf16),
            pltpu.VMEM((line // 16, LANES), f32),
            pltpu.VMEM((grps, line // 16, LANES), f32),
            pltpu.VMEM((8, line), f32),
            pltpu.VMEM((grps, 8, line), f32),
            pltpu.VMEM((rows, cols), f32),
            pltpu.VMEM((grps, rows, cols), f32),
            pltpu.VMEM((olev + 1, rows + 16, cols + 2 * LANES), f32),
            pltpu.VMEM((lons, parts * lat_count, LANES), f32),
            pltpu.VMEM((lons, parts * lat_count, LANES), bf16),
            pltpu.VMEM((lons, parts * lat_count, LANES), bf16),
            pltpu.VMEM((lats, parts * lat_count, LANES), bf16),
            pltpu.VMEM((lats // 2, m_local, lat_count * n_local), bf16),
            pltpu.VMEM((lats, m_local, lat_count * n_local), bf16),
            pltpu.VMEM((parts * m_local, lat_count * n_local), f32),
            dmas(6),
            dma,
            dmas(lats),
            dmas(lat_per),
            dma,
            dmas(grps),
            dmas(lons),
            dmas(lon_per),
            dmas(lons),
            dmas(lons),
            dmas(lats),
            dmas(lats),
            dmas(grps),
            dmas(grps),
            dma,
            dmas(grps),
            dmas(8),
            dmas(8),
            dmas(lons),
            dmas(lons),
            dmas(lats),
            dmas(lats),
            dmas(lats // 2),
            dmas(lats),
            dmas(lats // 2),
            dmas(lats),
        ],
        compiler_params=pltpu.CompilerParams(
            collective_id=0, has_side_effects=True, vmem_limit_bytes=VMEM_LIMIT
        ),
    )(
        parallel_nodes,
        layer_pressure_share,
        layer_sensitivity,
        associated_polynomial_quadrature,
        skin_warmth_mapping_factors.reshape(-1, block_air, cols),
        cool_factors.reshape(-1, cool_ways, cols),
        aloft_gridpoint,
        marine_heat,
        water_indicator,
        warm_ids,
        cool_ids,
    )
    spectra = spec[:, : parts * m_local].reshape(n_local, parts, m_local)
    return (spectra, ocean)


def solution(mesh):
    in_specs = (
        P("grp", "lat", "lon"),
        P("lat"),
        P("grp"),
        P("grp"),
        P("lat", "lon", None),
        P("grp", "lat", "lon"),
        P("lat", "lon"),
        P("lat", "lon", None),
        P("lat", "lon", None, None, None),
        P("lat", "lon", None),
        P("lat", "lon", None, None, None),
    )
    out_specs = (P("lat", "grp", "lon"), P("grp", "lat", "lon"))
    return jax.shard_map(
        per_device, mesh=mesh, in_specs=in_specs, out_specs=out_specs, check_vma=False
    )
```

```python
import functools
import math

import jax
import jax.numpy as jnp
from jax import lax
from jax.experimental import pallas as pl
from jax.experimental.pallas import tpu as pltpu
from jax.sharding import PartitionSpec as P

TWO_PI = 6.283185307179586
FLUX_RATE = 0.5
KAPPA = 0.2
MESH_ID = pl.DeviceIdType.MESH
LANES = 128
BLK_PAD = 64
VMEM_LIMIT = 48 * 1024 * 1024


def shifted(index, offset, count):
    return lax.rem(index + offset, count)


def greet(partners, sometimes, extra):
    barrier = pltpu.get_barrier_semaphore()
    for partner in partners:
        pl.semaphore_signal(barrier, inc=1, device_id=partner, device_id_type=MESH_ID)
    for needed, partner in sometimes:
        @pl.when(needed)
        def _(partner=partner):
            pl.semaphore_signal(barrier, inc=1, device_id=partner, device_id_type=MESH_ID)

    return len(partners) + extra


def remote(src, dst, send_sem, recv_sem, partner):
    return pltpu.make_async_remote_copy(
        src_ref=src,
        dst_ref=dst,
        send_sem=send_sem,
        recv_sem=recv_sem,
        device_id=partner,
        device_id_type=MESH_ID,
    )


def landed(ref, sem):
    pltpu.make_async_copy(ref, ref, sem).wait()


def turn(phase, count, inverse):
    rest = phase - jnp.floor(phase * inverse + 0.5) * count
    part = rest * inverse
    square = part * part
    cosine = jnp.zeros_like(part)
    sine = jnp.zeros_like(part)
    for power in range(8, -1, -1):
        sign = -1.0 if power % 2 else 1.0
        cosine = cosine * square + sign * TWO_PI ** (2 * power) / math.factorial(2 * power)
        sine = sine * square - sign * TWO_PI ** (2 * power + 1) / math.factorial(2 * power + 1)
    return cosine, sine * part


def step_kernel(
    sizes,
    nodes_hbm,
    share_hbm,
    sens_hbm,
    quad_hbm,
    warm_hbm,
    cool_hbm,
    aloft_raw_ref,
    heat_ref,
    water_ref,
    warm_raw_ref,
    cool_raw_ref,
    spec_ref,
    ocean_ref,
    nodes_ref,
    share_ref,
    sens_ref,
    quad_ref,
    warm_ref,
    cool_ref,
    sea_ref,
    flux_ref,
    e1_ref,
    e2_ref,
    warm_rows,
    picked_ref,
    aloft_ref,
    warm_ids_ref,
    cool_ids_ref,
    stage,
    part,
    gathered,
    warmth_out,
    warmth_in,
    flux_out,
    flux_in,
    ext,
    sea_waves,
    waves,
    waves_out,
    waves_in,
    fourier,
    quad_out,
    quad_in,
    sums,
    local_sems,
    own_sem,
    sea1_send,
    sea1_recv,
    flux0_send,
    flux0_recv,
    flux1_send,
    flux1_recv,
    sea2_send,
    sea2_recv,
    flux2_send,
    flux2_recv,
    warmth_send,
    warmth_recv,
    fluxp_send,
    fluxp_recv,
    halo_send,
    halo_recv,
    waves_send,
    waves_recv,
    fourier_send,
    fourier_recv,
    quad_send,
    quad_recv,
    beside_send,
    across_send,
    again_send,
    pass_recv,
):
    (grps, lats, lons, lat_count, levels, lon_local, block_air, m_local, degrees, olev, rows, cols) = sizes
    g, t, y = (lax.axis_index(name) for name in ("grp", "lat", "lon"))
    f32, bf16, i32 = jnp.float32, jnp.bfloat16, jnp.int32
    wide = lons * LANES
    blocks = lon_local // block_air
    parts = 2 * levels
    n_local = degrees // lats
    line = lat_count * BLK_PAD
    lon_per, lat_per = lons // grps, lats // grps
    flux_owner, yy = y // lon_per, lax.rem(y, lon_per)
    sea_owner, tt = lax.rem(t, grps), t // grps
    core = lax.rem(g, 2)
    beside = g + 1 - 2 * core
    across = lax.rem(g + 2, grps)
    beyond = across + 1 - 2 * core
    north, south = shifted(t, lats - 1, lats), shifted(t, 1, lats)
    west, east = shifted(y, lons - 1, lons), shifted(y, 1, lons)
    mid_rows, mid_cols = slice(8, 8 + rows), slice(LANES, LANES + cols)
    first_rows, last_rows = slice(8, 16), slice(rows, rows + 8)
    low_rows, high_rows = slice(0, 8), slice(8 + rows, 16 + rows)
    low_cols, high_cols = slice(0, LANES), slice(LANES + cols, 2 * LANES + cols)
    halo = [
        ({"lat": south}, last_rows, low_rows, mid_cols),
        ({"lat": north}, first_rows, high_rows, mid_cols),
        ({"lon": east}, mid_rows, mid_rows, low_cols),
        ({"lon": west}, mid_rows, mid_rows, high_cols),
        ({"lat": south, "lon": east}, last_rows, low_rows, low_cols),
        ({"lat": south, "lon": west}, last_rows, low_rows, high_cols),
        ({"lat": north, "lon": east}, first_rows, high_rows, low_cols),
        ({"lat": north, "lon": west}, first_rows, high_rows, high_cols),
    ]
    turns = lats // grps

    fetches = [
        pltpu.make_async_copy(src, dst, local_sems.at[k])
        for k, (src, dst) in enumerate(
            (
                (nodes_hbm, nodes_ref),
                (share_hbm, share_ref),
                (sens_hbm, sens_ref),
                (quad_hbm, quad_ref),
                (cool_hbm, cool_ref),
                (warm_hbm, warm_ref),
            )
        )
    ]
    for fetch in fetches:
        fetch.start()

    stage[...] = heat_ref[0].astype(bf16)
    expected = jnp.where(g == 0, jnp.where(sea_owner == 0, lats - 1, lats), 0)
    keepers = [(k * grps + g, {"grp": jnp.int32(0), "lat": k * grps + g}) for k in range(lat_per)]
    awaited = greet(
        [{"grp": shifted(g, d, grps)} for d in range(1, grps)]
        + [{"lon": shifted(y, d, lons)} for d in range(1, lons)]
        + [{"lat": shifted(t, d, lats)} for d in range(1, lats)]
        + [partner for partner, _, _, _ in halo[4:]],
        [((g != 0) | (at != t), partner) for at, partner in keepers],
        expected,
    )

    def distance(rank):
        half = jnp.where(rank % 2 == 1, (rank + 1) // 2, turns - rank // 2)
        return grps * lax.rem(half, turns)

    def source(rank, member):
        return shifted(t, lats - distance(rank) - member, lats)

    def pack(rank, carry):
        other = shifted(t, distance(rank) + g, lats)
        start = other * n_local
        first = jnp.minimum(start // LANES, degrees // LANES - 2)
        offset = start - first * LANES
        lanes = pl.ds(pl.multiple_of(first * LANES, LANES), 2 * LANES)
        at = lax.broadcasted_iota(i32, (16, 2 * LANES), 1)

        def some_rows(b, inner_carry):
            own = pl.ds(pl.multiple_of(b * 16, 16), 16)
            out = [jnp.zeros((16, LANES), f32) for _ in range(lat_count * n_local // LANES + 1)]
            for i in range(lat_count):
                tile, inner = divmod(i * n_local, LANES)
                window = quad_ref[i, own, lanes].astype(f32)
                window = pltpu.roll(window, lax.rem(inner - offset + 2 * LANES, 2 * LANES), 1)
                window = jnp.where((at >= inner) & (at < inner + n_local), window, 0.0)
                out[tile] = out[tile] + window[:, :LANES]
                if inner + n_local > LANES:
                    out[tile + 1] = out[tile + 1] + window[:, LANES:]
            for k in range(lat_count * n_local // LANES):
                quad_out[rank, own, k * LANES : (k + 1) * LANES] = out[k].astype(bf16)
            return inner_carry

        lax.fori_loop(0, m_local // 16, some_rows, 0)
        return carry

    own_copy = pltpu.make_async_copy(quad_out.at[0], quad_in.at[t], own_sem)

    def send_packed(rank, carry):
        @pl.when((rank == 0) & (g == 0))
        def _():
            own_copy.start()

        @pl.when((rank != 0) | (g != 0))
        def _():
            remote(
                quad_out.at[rank],
                quad_in.at[t],
                quad_send.at[rank],
                quad_recv.at[t],
                {"lat": shifted(t, distance(rank) + g, lats)},
            ).start()

        return carry

    def pass_on(rank, carry):
        s = source(rank, g)

        @pl.when((rank == 0) & (g == 0))
        def _():
            own_copy.wait()

        @pl.when((rank != 0) | (g != 0))
        def _():
            landed(quad_in.at[s], quad_recv.at[s])

        remote(
            quad_in.at[s], quad_in.at[s], beside_send.at[rank], pass_recv.at[s], {"grp": beside}
        ).start()
        remote(
            quad_in.at[s], quad_in.at[s], across_send.at[rank], pass_recv.at[s], {"grp": across}
        ).start()
        return carry

    def pass_again(rank, carry):
        s = source(rank, across)
        landed(quad_in.at[s], pass_recv.at[s])
        remote(
            quad_in.at[s], quad_in.at[s], again_send.at[rank], pass_recv.at[s], {"grp": beside}
        ).start()
        return carry

    fetches[3].wait()
    lax.fori_loop(0, turns // 2, pack, 0)
    pl.semaphore_wait(pltpu.get_barrier_semaphore(), awaited)

    @pl.when(g == 0)
    def _():
        for d in range(1, lats):
            remote(
                stage,
                sea_ref.at[y, tt],
                sea1_send.at[d],
                sea1_recv.at[tt],
                {"grp": sea_owner, "lat": shifted(t, d, lats)},
            ).start()

    @pl.when((g == 0) & (sea_owner != 0))
    def _():
        remote(
            stage, sea_ref.at[y, tt], sea1_send.at[0], sea1_recv.at[tt], {"grp": sea_owner}
        ).start()

    @pl.when((g == 0) & (sea_owner == 0))
    def _():
        sea_ref[y, tt] = stage[...]

    lax.fori_loop(0, turns // 2, send_packed, 0)
    lax.fori_loop(turns // 2, turns, pack, 0)
    lax.fori_loop(turns // 2, turns, send_packed, 0)

    for fetch in fetches[:3]:
        fetch.wait()
    tiles = line // LANES
    raw = jnp.concatenate([aloft_raw_ref[l].astype(f32) for l in range(levels)], axis=0)
    source_id = lax.broadcasted_iota(i32, (lon_local, 8 * BLK_PAD), 0)
    target_id = lax.broadcasted_iota(i32, (lon_local, 8 * BLK_PAD), 1)
    target_block, target_slot = target_id % BLK_PAD, target_id // BLK_PAD
    sorting = jnp.where(
        (target_block < blocks)
        & (target_slot < block_air)
        & (source_id == target_block * block_air + target_slot),
        1.0,
        0.0,
    ).astype(bf16)
    by_slot = jnp.dot(raw.astype(bf16), sorting, preferred_element_type=f32)
    aloft_ref[...] = jnp.zeros_like(aloft_ref)
    out_lane = lax.broadcasted_iota(i32, (8, LANES), 1)
    out_row = lax.broadcasted_iota(i32, (8, LANES), 0)
    for l in range(levels):
        for q in range(block_air):
            k = q // 2
            two = by_slot[8 * l : 8 * l + 8, k * LANES : (k + 1) * LANES]
            other = pltpu.roll(two, BLK_PAD, 1)
            both = jnp.where((out_lane < BLK_PAD) == (q % 2 == 0), two, other)
            for k in range(tiles):
                mine = out_row == 2 * k + out_lane // BLK_PAD
                aloft_ref[8 * l + q : 8 * l + q + 1, k * LANES : (k + 1) * LANES] = jnp.sum(
                    jnp.where(mine, both, 0.0), axis=0, keepdims=True
                )
    lane = lax.broadcasted_iota(i32, (8, line), 1)
    slot = lax.broadcasted_iota(i32, (8, line), 0)
    block = lane % BLK_PAD
    limit = jnp.zeros((8, line), i32)
    for i in range(lat_count):
        limit = jnp.where(lane // BLK_PAD == i, nodes_ref[i], limit)
    live = (block < blocks) & (slot < block_air)
    live = live & (y * lon_local + block * block_air + slot < limit)
    flux_sum = share_ref[0] * aloft_ref[0:8, :]
    for l in range(1, levels):
        flux_sum = flux_sum + share_ref[l] * aloft_ref[8 * l : 8 * l + 8, :]
    flux_sum = jnp.where(live, flux_sum, 0.0)
    for k in range(tiles):
        part[8 * k : 8 * k + 8, :] = flux_sum[:, k * LANES : (k + 1) * LANES]

    @pl.when(g != flux_owner)
    def _():
        remote(
            part, gathered.at[g], flux0_send, flux0_recv.at[g], {"grp": flux_owner}
        ).start()

    for r in range(lat_per):
        nearest = (t - g + lats) // grps
        k = lax.rem(nearest + lats + ((r + 1) // 2 if r % 2 else -(r // 2)), lat_per)

        @pl.when((g != 0) | (k * grps + g != t))
        def _():
            landed(sea_ref.at[y, k], sea1_recv.at[k])

        for d in range(1, lons):
            remote(
                sea_ref.at[y, k],
                sea_ref.at[y, k],
                sea2_send.at[d * lat_per + r],
                sea2_recv.at[y * lat_per + k],
                {"lon": shifted(y, d, lons)},
            ).start()

    for level in range(olev):
        ext[level, mid_rows, mid_cols] = heat_ref[level]
    wet_mid = water_ref[...].astype(f32)
    ext[olev, mid_rows, mid_cols] = wet_mid

    def tables(i, carry):
        count = jnp.full((8, LANES), nodes_ref[i], i32).astype(f32)
        inverse = jnp.concatenate([1.0 / count] * lons, axis=1)
        count = jnp.concatenate([count] * lons, axis=1)
        lane = lax.broadcasted_iota(i32, (8, wide), 1)
        row_f = lax.broadcasted_iota(i32, (8, wide), 0).astype(f32)
        inner = lane % LANES
        wave_f = ((lane // LANES) * m_local + inner).astype(f32)
        base_f = (y * lon_local).astype(f32)
        high = turn((base_f + 8 * block_air * row_f) * wave_f, count, inverse)
        low = turn((block_air * row_f) * wave_f, count, inverse)
        fine = turn(row_f * wave_f, count, inverse)
        usable = (inner < m_local) & (2.0 * wave_f < count)
        own = pl.ds(pl.multiple_of(i * 8, 8), 8)
        e2_ref[own, :wide] = jnp.where(usable, fine[0] * inverse, 0.0)
        e2_ref[own, wide:] = jnp.where(usable, fine[1] * inverse, 0.0)
        for pair in range(BLK_PAD // 16):
            real, imag = [], []
            for b in (2 * pair, 2 * pair + 1):
                hr, hi = high[0][b : b + 1], high[1][b : b + 1]
                real.append(hr * low[0] - hi * low[1])
                imag.append(hr * low[1] + hi * low[0])
            where = pl.ds(pl.multiple_of(i * BLK_PAD + pair * 16, 16), 16)
            e1_ref[where, :wide] = jnp.concatenate(real, axis=0).astype(bf16)
            e1_ref[where, wide:] = jnp.concatenate(imag, axis=0).astype(bf16)
        return carry

    lax.fori_loop(0, lat_count // 2, tables, 0)

    @pl.when(g == flux_owner)
    def _():
        gathered[g] = part[...]
        for d in range(1, grps):
            other = shifted(g, d, grps)
            landed(gathered.at[other], flux0_recv.at[other])
        total = gathered[0]
        for other in range(1, grps):
            total = total + gathered[other]
        flux_ref[t, yy] = total.astype(bf16)
        for d in range(1, lons):
            remote(
                flux_ref.at[t, yy],
                flux_ref.at[t, yy],
                flux1_send.at[d],
                flux1_recv.at[yy],
                {"lon": shifted(y, d, lons)},
            ).start()

    lax.fori_loop(lat_count // 2, lat_count, tables, 0)

    picks = 2 * blocks
    fill = jnp.zeros((picks, 8 - block_air, LANES), f32)
    fetches[5].wait()

    def prepare(i, carry):
        factor = warm_ref[pl.ds(i * picks, picks)].astype(f32)
        factor = jnp.concatenate([factor, fill], axis=1).reshape(picks * 8, LANES)
        warm_rows[i] = factor.astype(bf16)
        return carry

    lax.fori_loop(0, lat_count, prepare, 0)
    warm_ids_ref[...] = jnp.full_like(warm_ids_ref, -1)
    for i in range(lat_count):
        for k in range(warm_raw_ref.shape[1]):
            warm_ids_ref[i : i + 1, k * BLK_PAD : k * BLK_PAD + blocks] = warm_raw_ref[
                i, k : k + 1, :
            ]
    chosen = warm_ids_ref[...]
    column, row = chosen % lons, chosen // lons
    band = row // rows
    spot = (band // grps) * rows + row % rows
    spot = jnp.where((band % grps == g) & (chosen >= 0), spot + column * LANES, -1)
    spot = jnp.concatenate([spot[i : i + 1] for i in range(lat_count)], axis=1)
    table_row = lax.broadcasted_iota(i32, (LANES, lat_count * LANES), 0)

    lax.fori_loop(0, turns // 2, pass_on, 0)

    def pick_chunk(r, carry):
        other = lax.rem(y + lons + jnp.where(r % 2 == 1, (r + 1) // 2, -(r // 2)), lons)

        @pl.when(other != y)
        def _():
            for k in range(lat_per):
                landed(sea_ref.at[other, k], sea2_recv.at[other * lat_per + k])

        chunk = jnp.transpose(sea_ref[other].reshape(LANES, cols).astype(f32)).astype(bf16)
        one_hot = jnp.where(table_row == spot - other * LANES, 1.0, 0.0).astype(bf16)
        found = jnp.dot(chunk, one_hot, preferred_element_type=f32)
        picked_ref[...] = jnp.where(r == 0, found, picked_ref[...] + found)
        return carry

    picked_ref[...] = jnp.zeros_like(picked_ref)
    lax.fori_loop(0, lons, pick_chunk, 0)
    pick_id = lax.broadcasted_iota(i32, (picks, 8, LANES), 0)
    pick_lane = lax.broadcasted_iota(i32, (picks, 8, LANES), 2)
    diagonal = pick_lane == (pick_id % 2) * BLK_PAD + pick_id // 2
    warm_sums = []
    for i in range(lat_count):
        picked = picked_ref[:, i * LANES : (i + 1) * LANES].astype(bf16)
        product = jnp.dot(warm_rows[i], picked, preferred_element_type=f32)
        product = product.reshape(picks, 8, LANES)
        total = jnp.sum(jnp.where(diagonal, product, 0.0), axis=0)
        warm_sums.append(total + pltpu.roll(total, BLK_PAD, 1))
    for k in range(tiles):
        warmth_out[:, k * LANES : (k + 1) * LANES] = jnp.where(
            out_lane < BLK_PAD, warm_sums[2 * k], warm_sums[2 * k + 1]
        )
    for d in range(1, grps):
        remote(
            warmth_out,
            warmth_in.at[g],
            warmth_send.at[d],
            warmth_recv.at[g],
            {"grp": shifted(g, d, grps)},
        ).start()

    for k in range(lon_per):
        @pl.when(g * lon_per + k != y)
        def _():
            landed(flux_ref.at[t, k], flux1_recv.at[k])

    for d in range(1, lats):
        remote(
            flux_ref.at[t],
            flux_ref.at[t],
            flux2_send.at[d],
            flux2_recv.at[t],
            {"lat": shifted(t, d, lats)},
        ).start()

    def transform(field, count, out_ref):
        lane = lax.broadcasted_iota(i32, field.shape, 1)
        stacked = jnp.concatenate(
            [jnp.where(lane // BLK_PAD == i, field, 0.0) for i in range(lat_count)], axis=0
        ).astype(bf16)
        real = jnp.dot(stacked, e1_ref[:, :wide], preferred_element_type=f32)
        imag = jnp.dot(stacked, e1_ref[:, wide:], preferred_element_type=f32)
        for i in range(lat_count):
            slot_r = e2_ref[8 * i : 8 * i + 8, :wide]
            slot_i = e2_ref[8 * i : 8 * i + 8, wide:]
            for l in range(count):
                at = (i * count + l) * 8
                re, im = real[at : at + 8], imag[at : at + 8]
                out_r = jnp.sum(re * slot_r - im * slot_i, axis=0, keepdims=True)
                out_i = jnp.sum(re * slot_i + im * slot_r, axis=0, keepdims=True)
                for c, out in enumerate((out_r, out_i)):
                    row = (2 * l + c) * lat_count + i
                    for k in range(lons):
                        out_ref[k, row : row + 1, :] = out[:, k * LANES : (k + 1) * LANES]

    transform(
        jnp.concatenate(
            [jnp.where(live, aloft_ref[8 * l : 8 * l + 8, :], 0.0) for l in range(levels)], axis=0
        ),
        levels,
        waves,
    )
    lax.fori_loop(turns // 2, turns, pass_on, 0)
    warmth = warmth_out[...]
    for d in range(1, grps):
        other = shifted(g, d, grps)
        landed(warmth_in.at[other], warmth_recv.at[other])
        warmth = warmth + warmth_in[other]
    transform(jnp.where(live, warmth, 0.0), 1, sea_waves)
    for l in range(levels):
        at = slice(2 * l * lat_count, 2 * (l + 1) * lat_count)
        waves[:, at, :] = waves[:, at, :] + sens_ref[l] * sea_waves[...]
    waves_out[...] = waves[...].astype(bf16)
    for d in range(1, lons):
        other = shifted(y, d, lons)
        remote(
            waves_out.at[other],
            waves_in.at[y],
            waves_send.at[d],
            waves_recv.at[y],
            {"lon": other},
        ).start()

    for d in range(1, lats):
        other = shifted(t, d, lats)
        landed(flux_ref.at[other], flux2_recv.at[other])
    ways = cool_raw_ref.shape[0]
    for k in range(ways):
        cool_ids_ref[0:1, k * rows : (k + 1) * rows] = cool_raw_ref[k : k + 1, :]
    chosen = cool_ids_ref[0:1, :]
    parallel, place = chosen // (blocks * lons), chosen % (blocks * lons)
    band, within = parallel // lat_count, parallel % lat_count
    lon, blk = place // blocks, place % blocks
    group = (band * lon_per + lon % lon_per) * tiles + within // 2
    group = jnp.where(lon // lon_per == g, group, -1)
    spot = (within % 2) * BLK_PAD + blk
    group_count = lats * lon_per * tiles
    one_hot = jnp.where(
        lax.broadcasted_iota(i32, (LANES, LANES), 0) == spot, 1.0, 0.0
    ).astype(bf16)
    found = jnp.dot(
        flux_ref[...].reshape(group_count * 8, LANES), one_hot, preferred_element_type=f32
    ).reshape(group_count, 8, LANES)
    group_id = lax.broadcasted_iota(i32, (group_count, 8, LANES), 0)
    air = jnp.sum(jnp.where(group_id == group[None], found, 0.0), axis=0)
    width = rows * block_air * 8
    to = lax.broadcasted_iota(i32, (LANES, width), 1)
    repeat = jnp.where(
        (to % 8 < ways)
        & (lax.broadcasted_iota(i32, (LANES, width), 0) == (to % 8) * rows + to // (8 * block_air)),
        1.0,
        0.0,
    ).astype(bf16)
    air = jnp.dot(air.astype(bf16), repeat, preferred_element_type=f32)
    to = lax.broadcasted_iota(i32, (8, width), 1)
    own_slot = (to // 8) % block_air == lax.broadcasted_iota(i32, (8, width), 0)
    air = jnp.sum(jnp.where(own_slot, air, 0.0), axis=0, keepdims=True)
    air = jnp.where(
        lax.broadcasted_iota(i32, (rows, width), 1) // (8 * block_air)
        == lax.broadcasted_iota(i32, (rows, width), 0),
        air,
        0.0,
    ).astype(bf16)
    fetches[4].wait()
    factor = cool_ref[...].astype(f32)
    factor = jnp.concatenate(
        [factor, jnp.zeros((rows * block_air, 8 - ways, LANES), f32)], axis=1
    ).reshape(width, LANES)
    flux_out[...] = jnp.dot(air, factor.astype(bf16), preferred_element_type=f32)

    @pl.when(g != 0)
    def _():
        remote(
            flux_out, flux_in.at[g], fluxp_send, fluxp_recv.at[g], {"grp": jnp.int32(0)}
        ).start()

    lax.fori_loop(0, turns // 2, pass_again, 0)

    total = waves[y]
    for d in range(1, lons):
        other = shifted(y, d, lons)
        landed(waves_in.at[other], waves_recv.at[other])
        total = total + waves_in[other].astype(f32)
    fourier[t] = total.astype(bf16)

    def send_fourier(offset):
        @pl.when(offset != 0)
        def _():
            remote(
                fourier.at[t],
                fourier.at[t],
                fourier_send.at[offset],
                fourier_recv.at[t],
                {"lat": shifted(t, offset, lats)},
            ).start()

    def send_some(rank, carry):
        for member in range(grps):
            send_fourier(distance(rank) + member)
        return carry

    lax.fori_loop(0, turns, send_some, 0)

    @pl.when(g == 0)
    def _():
        total = flux_out[...]
        for other in range(1, grps):
            landed(flux_in.at[other], fluxp_recv.at[other])
            total = total + flux_in[other]
        ext[0, mid_rows, mid_cols] = heat_ref[0] + FLUX_RATE * total * wet_mid

    for index, (partner, src_rows, dst_rows, dst_cols) in enumerate(halo):
        remote(
            ext.at[:, src_rows, mid_cols],
            ext.at[:, dst_rows, dst_cols],
            halo_send.at[index],
            halo_recv.at[index],
            partner,
        ).start()

    lax.fori_loop(turns // 2, turns, pass_again, 0)

    span = lat_count * n_local
    repeat_row = lax.broadcasted_iota(i32, (LANES, span), 0)
    repeat = jnp.where(
        (repeat_row < parts * lat_count)
        & (repeat_row % lat_count == lax.broadcasted_iota(i32, (LANES, span), 1) // n_local),
        1.0,
        0.0,
    ).astype(bf16)
    fill = jnp.zeros((LANES - parts * lat_count, LANES), f32)
    part_lane = lax.broadcasted_iota(i32, (m_local, LANES), 1) // lat_count
    sums[...] = jnp.zeros_like(sums)

    def coefficients(s):
        @pl.when(s != t)
        def _():
            landed(fourier.at[s], fourier_recv.at[s])

        columns = jnp.transpose(jnp.concatenate([fourier[s].astype(f32), fill], axis=0))[:m_local]
        own = jnp.concatenate(
            [jnp.where(part_lane == a, columns, 0.0) for a in range(parts)], axis=0
        ).astype(bf16)
        return jnp.dot(own, repeat, preferred_element_type=f32)

    def add_two(first, second):
        coefs = coefficients(first), coefficients(second)
        quads = quad_in[first].astype(f32), quad_in[second].astype(f32)
        for a in range(parts):
            at = slice(a * m_local, (a + 1) * m_local)
            sums[at, :] = sums[at, :] + coefs[0][at] * quads[0] + coefs[1][at] * quads[1]

    def add_some(rank, carry):
        add_two(source(rank, g), source(rank, across))
        for member in (beside, beyond):
            s = source(rank, member)
            landed(quad_in.at[s], pass_recv.at[s])
        add_two(source(rank, beside), source(rank, beyond))
        return carry

    lax.fori_loop(0, 3 * turns // 4, add_some, 0)

    for index, (partner, src_rows, dst_rows, dst_cols) in enumerate(halo):
        landed(ext.at[:, dst_rows, dst_cols], halo_recv.at[index])
    shape = (rows + 16, cols + 2 * LANES)
    row_id = lax.broadcasted_iota(i32, shape, 0) + (t * rows - 8)
    col_id = lax.broadcasted_iota(i32, shape, 1) + (y * cols - LANES)
    inside = (row_id >= 0) & (row_id < rows * lats) & (col_id >= 0) & (col_id < cols * lons)
    wet = jnp.where(inside, ext[olev], 0.0)
    moves = ((1, 0), (shape[0] - 1, 0), (1, 1), (shape[1] - 1, 1))
    wet_near = [pltpu.roll(wet, shift, axis) for shift, axis in moves]
    for level in range(olev):
        field = ext[level]
        for _ in range(2):
            total = jnp.zeros_like(field)
            for (shift, axis), near in zip(moves, wet_near):
                total = total + near * (pltpu.roll(field, shift, axis) - field)
            field = field + KAPPA * wet * total
        ocean_ref[level] = field[mid_rows, mid_cols]

    lax.fori_loop(3 * turns // 4, turns, add_some, 0)

    folded = jnp.zeros((parts * m_local, LANES), f32)
    for i in range(lat_count):
        tile, inner = divmod(i * n_local, LANES)
        if inner + n_local > LANES:
            window = sums[:, tile * LANES : (tile + 2) * LANES]
            folded = folded + pltpu.roll(window, 2 * LANES - inner, 1)[:, :LANES]
        else:
            window = sums[:, tile * LANES : (tile + 1) * LANES]
            folded = folded + (pltpu.roll(window, LANES - inner, 1) if inner else window)
    width = spec_ref.shape[1]
    folded = jnp.concatenate(
        [folded, jnp.zeros((width - parts * m_local, LANES), f32)], axis=0
    )
    result = jnp.transpose(folded)[:n_local]
    lane = lax.broadcasted_iota(i32, result.shape, 1)
    degree = lax.broadcasted_iota(i32, result.shape, 0) + t * n_local
    spec_ref[...] = jnp.where(degree >= lane % m_local + y * m_local, result, 0.0)

    @pl.when(g == 0)
    def _():
        for d in range(1, lats):
            landed(stage, sea1_send.at[d])

    @pl.when((g == 0) & (sea_owner != 0))
    def _():
        landed(stage, sea1_send.at[0])

    @pl.when(g != flux_owner)
    def _():
        landed(part, flux0_send)

    @pl.when(g == flux_owner)
    def _():
        for d in range(1, lons):
            landed(flux_ref.at[t, yy], flux1_send.at[d])

    @pl.when(g != 0)
    def _():
        landed(flux_out, fluxp_send)

    for d in range(1, lats):
        landed(flux_ref.at[t], flux2_send.at[d])
        landed(fourier.at[t], fourier_send.at[d])
    for d in range(1, lons):
        for r in range(lat_per):
            landed(sea_ref.at[y, 0], sea2_send.at[d * lat_per + r])
        landed(waves_out.at[0], waves_send.at[d])
    for d in range(1, grps):
        landed(warmth_out, warmth_send.at[d])
    for index, (partner, src_rows, dst_rows, dst_cols) in enumerate(halo):
        landed(ext.at[:, src_rows, mid_cols], halo_send.at[index])

    def sent(rank, carry):
        @pl.when((rank != 0) | (g != 0))
        def _():
            landed(quad_out.at[rank], quad_send.at[rank])

        for sem in (beside_send, across_send, again_send):
            landed(quad_in.at[0], sem.at[rank])
        return carry

    lax.fori_loop(0, turns, sent, 0)


def per_device(
    aloft_gridpoint,
    parallel_nodes,
    layer_pressure_share,
    layer_sensitivity,
    associated_polynomial_quadrature,
    marine_heat,
    water_indicator,
    heat_feeding_panels,
    heat_transfer_factors,
    skin_warmth_feeding_panels,
    skin_warmth_mapping_factors,
):
    grps, lats, lons = (lax.axis_size(name) for name in ("grp", "lat", "lon"))
    levels, lat_count, lon_local = aloft_gridpoint.shape
    block_air = heat_transfer_factors.shape[3]
    blocks = lon_local // block_air
    olev, rows, cols = marine_heat.shape
    m_local, degrees = associated_polynomial_quadrature.shape[1:]
    lon_per, lat_per = lons // grps, lats // grps
    wide = lons * LANES
    line = lat_count * BLK_PAD
    parts = 2 * levels
    n_local = degrees // lats
    width = -(-parts * m_local // LANES) * LANES
    warm_ways = skin_warmth_feeding_panels.shape[2]
    cool_ways = heat_feeding_panels.shape[2]
    vmem = pl.BlockSpec(memory_space=pltpu.VMEM)
    hbm = pl.BlockSpec(memory_space=pl.ANY)
    f32, bf16 = jnp.float32, jnp.bfloat16
    dma, dmas = pltpu.SemaphoreType.DMA, lambda n: pltpu.SemaphoreType.DMA((n,))

    warm_ids = skin_warmth_feeding_panels.transpose(0, 2, 1)
    cool_ids = heat_feeding_panels[:, 0, :].transpose(1, 0)
    cool_factors = heat_transfer_factors.transpose(0, 1, 3, 2, 4)

    sizes = (
        grps, lats, lons, lat_count, levels, lon_local, block_air, m_local, degrees, olev, rows, cols
    )
    spec, ocean = pl.pallas_call(
        functools.partial(step_kernel, sizes),
        out_shape=(
            jax.ShapeDtypeStruct((n_local, width), f32),
            jax.ShapeDtypeStruct((olev, rows, cols), f32),
        ),
        in_specs=[hbm] * 6 + [vmem] * 5,
        out_specs=(vmem, vmem),
        scratch_shapes=[
            pltpu.SMEM((lat_count,), jnp.int32),
            pltpu.SMEM((levels,), f32),
            pltpu.SMEM((levels,), f32),
            pltpu.VMEM((lat_count, m_local, degrees), bf16),
            pltpu.VMEM((lat_count * blocks * warm_ways, block_air, cols), bf16),
            pltpu.VMEM((rows * block_air, cool_ways, cols), bf16),
            pltpu.VMEM((lons, lat_per, rows, cols), bf16),
            pltpu.VMEM((lats, lon_per, line // 16, LANES), bf16),
            pltpu.VMEM((line, 2 * wide), bf16),
            pltpu.VMEM((lat_count * 8, 2 * wide), f32),
            pltpu.VMEM((lat_count, blocks * warm_ways * 8, cols), bf16),
            pltpu.VMEM((cols, lat_count * LANES), f32),
            pltpu.VMEM((levels * 8, line), f32),
            pltpu.VMEM((lat_count, warm_ways * BLK_PAD), jnp.int32),
            pltpu.VMEM((8, rows * cool_ways), jnp.int32),
            pltpu.VMEM((rows, cols), bf16),
            pltpu.VMEM((line // 16, LANES), f32),
            pltpu.VMEM((grps, line // 16, LANES), f32),
            pltpu.VMEM((8, line), f32),
            pltpu.VMEM((grps, 8, line), f32),
            pltpu.VMEM((rows, cols), f32),
            pltpu.VMEM((grps, rows, cols), f32),
            pltpu.VMEM((olev + 1, rows + 16, cols + 2 * LANES), f32),
            pltpu.VMEM((lons, 2 * lat_count, LANES), f32),
            pltpu.VMEM((lons, parts * lat_count, LANES), f32),
            pltpu.VMEM((lons, parts * lat_count, LANES), bf16),
            pltpu.VMEM((lons, parts * lat_count, LANES), bf16),
            pltpu.VMEM((lats, parts * lat_count, LANES), bf16),
            pltpu.VMEM((lats // grps, m_local, lat_count * n_local), bf16),
            pltpu.VMEM((lats, m_local, lat_count * n_local), bf16),
            pltpu.VMEM((parts * m_local, lat_count * n_local), f32),
            dmas(6),
            dma,
            dmas(lats),
            dmas(lat_per),
            dma,
            dmas(grps),
            dmas(lons),
            dmas(lon_per),
            dmas(lons * lat_per),
            dmas(lons * lat_per),
            dmas(lats),
            dmas(lats),
            dmas(grps),
            dmas(grps),
            dma,
            dmas(grps),
            dmas(8),
            dmas(8),
            dmas(lons),
            dmas(lons),
            dmas(lats),
            dmas(lats),
            dmas(lats // grps),
            dmas(lats),
            dmas(lats // grps),
            dmas(lats // grps),
            dmas(lats // grps),
            dmas(lats),
        ],
        compiler_params=pltpu.CompilerParams(
            collective_id=0, has_side_effects=True, vmem_limit_bytes=VMEM_LIMIT
        ),
    )(
        parallel_nodes,
        layer_pressure_share,
        layer_sensitivity,
        associated_polynomial_quadrature,
        skin_warmth_mapping_factors.reshape(-1, block_air, cols),
        cool_factors.reshape(-1, cool_ways, cols),
        aloft_gridpoint,
        marine_heat,
        water_indicator,
        warm_ids,
        cool_ids,
    )
    spectra = spec[:, : parts * m_local].reshape(n_local, parts, m_local)
    return (spectra, ocean)


def solution(mesh):
    in_specs = (
        P("grp", "lat", "lon"),
        P("lat"),
        P("grp"),
        P("grp"),
        P("lat", "lon", None),
        P("grp", "lat", "lon"),
        P("lat", "lon"),
        P("lat", "lon", None),
        P("lat", "lon", None, None, None),
        P("lat", "lon", None),
        P("lat", "lon", None, None, None),
    )
    out_specs = (P("lat", "grp", "lon"), P("grp", "lat", "lon"))
    return jax.shard_map(
        per_device, mesh=mesh, in_specs=in_specs, out_specs=out_specs, check_vma=False
    )
```

```python
import functools
import math

import jax
import jax.numpy as jnp
from jax import lax
from jax.experimental import pallas as pl
from jax.experimental.pallas import tpu as pltpu
from jax.sharding import PartitionSpec as P

TWO_PI = 6.283185307179586
FLUX_RATE = 0.5
KAPPA = 0.2
MESH_ID = pl.DeviceIdType.MESH
LANES = 128
BLK_PAD = 64
VMEM_LIMIT = 48 * 1024 * 1024


def shifted(index, offset, count):
    return lax.rem(index + offset, count)


def greet(partners, sometimes, extra):
    barrier = pltpu.get_barrier_semaphore()
    for partner in partners:
        pl.semaphore_signal(barrier, inc=1, device_id=partner, device_id_type=MESH_ID)
    for needed, partner in sometimes:
        @pl.when(needed)
        def _(partner=partner):
            pl.semaphore_signal(barrier, inc=1, device_id=partner, device_id_type=MESH_ID)

    return len(partners) + extra


def remote(src, dst, send_sem, recv_sem, partner):
    return pltpu.make_async_remote_copy(
        src_ref=src,
        dst_ref=dst,
        send_sem=send_sem,
        recv_sem=recv_sem,
        device_id=partner,
        device_id_type=MESH_ID,
    )


def landed(ref, sem):
    pltpu.make_async_copy(ref, ref, sem).wait()


def turn(phase, count, inverse):
    rest = phase - jnp.floor(phase * inverse + 0.5) * count
    part = rest * inverse
    square = part * part
    cosine = jnp.zeros_like(part)
    sine = jnp.zeros_like(part)
    for power in range(8, -1, -1):
        sign = -1.0 if power % 2 else 1.0
        cosine = cosine * square + sign * TWO_PI ** (2 * power) / math.factorial(2 * power)
        sine = sine * square - sign * TWO_PI ** (2 * power + 1) / math.factorial(2 * power + 1)
    return cosine, sine * part


def step_kernel(
    sizes,
    nodes_hbm,
    share_hbm,
    sens_hbm,
    quad_hbm,
    warm_hbm,
    cool_hbm,
    aloft_raw_ref,
    heat_ref,
    water_ref,
    warm_raw_ref,
    cool_raw_ref,
    spec_ref,
    ocean_ref,
    nodes_ref,
    share_ref,
    sens_ref,
    quad_ref,
    warm_ref,
    cool_ref,
    sea_ref,
    flux_ref,
    e1_ref,
    e2_ref,
    warm_rows,
    picked_ref,
    aloft_ref,
    warm_ids_ref,
    cool_ids_ref,
    stage,
    part,
    gathered,
    warmth_out,
    warmth_in,
    flux_out,
    flux_in,
    ext,
    sea_waves,
    waves,
    waves_out,
    waves_in,
    fourier,
    quad_out,
    quad_in,
    sums,
    local_sems,
    own_sem,
    sea1_send,
    sea1_recv,
    flux0_send,
    flux0_recv,
    flux1_send,
    flux1_recv,
    sea2_send,
    sea2_recv,
    flux2_send,
    flux2_recv,
    warmth_send,
    warmth_recv,
    fluxp_send,
    fluxp_recv,
    halo_send,
    halo_recv,
    waves_send,
    waves_recv,
    fourier_send,
    fourier_recv,
    quad_send,
    quad_recv,
    beside_send,
    across_send,
    again_send,
    pass_recv,
):
    (grps, lats, lons, lat_count, levels, lon_local, block_air, m_local, degrees, olev, rows, cols) = sizes
    g, t, y = (lax.axis_index(name) for name in ("grp", "lat", "lon"))
    f32, bf16, i32 = jnp.float32, jnp.bfloat16, jnp.int32
    wide = lons * LANES
    blocks = lon_local // block_air
    parts = 2 * levels
    n_local = degrees // lats
    line = lat_count * BLK_PAD
    lon_per, lat_per = lons // grps, lats // grps
    flux_owner, yy = y // lon_per, lax.rem(y, lon_per)
    sea_owner, tt = lax.rem(t, grps), t // grps
    core = lax.rem(g, 2)
    beside = g + 1 - 2 * core
    across = lax.rem(g + 2, grps)
    beyond = across + 1 - 2 * core
    north, south = shifted(t, lats - 1, lats), shifted(t, 1, lats)
    west, east = shifted(y, lons - 1, lons), shifted(y, 1, lons)
    mid_rows, mid_cols = slice(8, 8 + rows), slice(LANES, LANES + cols)
    first_rows, last_rows = slice(8, 16), slice(rows, rows + 8)
    low_rows, high_rows = slice(0, 8), slice(8 + rows, 16 + rows)
    low_cols, high_cols = slice(0, LANES), slice(LANES + cols, 2 * LANES + cols)
    halo = [
        ({"lat": south}, last_rows, low_rows, mid_cols),
        ({"lat": north}, first_rows, high_rows, mid_cols),
        ({"lon": east}, mid_rows, mid_rows, low_cols),
        ({"lon": west}, mid_rows, mid_rows, high_cols),
        ({"lat": south, "lon": east}, last_rows, low_rows, low_cols),
        ({"lat": south, "lon": west}, last_rows, low_rows, high_cols),
        ({"lat": north, "lon": east}, first_rows, high_rows, low_cols),
        ({"lat": north, "lon": west}, first_rows, high_rows, high_cols),
    ]
    turns = lats // grps

    fetches = [
        pltpu.make_async_copy(src, dst, local_sems.at[k])
        for k, (src, dst) in enumerate(
            (
                (nodes_hbm, nodes_ref),
                (share_hbm, share_ref),
                (sens_hbm, sens_ref),
                (quad_hbm, quad_ref),
                (cool_hbm, cool_ref),
                (warm_hbm, warm_ref),
            )
        )
    ]
    for fetch in fetches:
        fetch.start()

    stage[...] = heat_ref[0].astype(bf16)
    expected = jnp.where(g == 0, jnp.where(sea_owner == 0, lats - 1, lats), 0)
    keepers = [(k * grps + g, {"grp": jnp.int32(0), "lat": k * grps + g}) for k in range(lat_per)]
    awaited = greet(
        [{"grp": shifted(g, d, grps)} for d in range(1, grps)]
        + [{"lon": shifted(y, d, lons)} for d in range(1, lons)]
        + [{"lat": shifted(t, d, lats)} for d in range(1, lats)]
        + [partner for partner, _, _, _ in halo[4:]],
        [((g != 0) | (at != t), partner) for at, partner in keepers],
        expected,
    )

    def distance(rank):
        half = jnp.where(rank % 2 == 1, (rank + 1) // 2, turns - rank // 2)
        return grps * lax.rem(half, turns)

    def source(rank, member):
        return shifted(t, lats - distance(rank) - member, lats)

    def pack(rank, carry):
        other = shifted(t, distance(rank) + g, lats)
        start = other * n_local
        first = jnp.minimum(start // LANES, degrees // LANES - 2)
        offset = start - first * LANES
        lanes = pl.ds(pl.multiple_of(first * LANES, LANES), 2 * LANES)
        at = lax.broadcasted_iota(i32, (16, 2 * LANES), 1)

        def some_rows(b, inner_carry):
            own = pl.ds(pl.multiple_of(b * 16, 16), 16)
            out = [jnp.zeros((16, LANES), f32) for _ in range(lat_count * n_local // LANES + 1)]
            for i in range(lat_count):
                tile, inner = divmod(i * n_local, LANES)
                window = quad_ref[i, own, lanes].astype(f32)
                window = pltpu.roll(window, lax.rem(inner - offset + 2 * LANES, 2 * LANES), 1)
                window = jnp.where((at >= inner) & (at < inner + n_local), window, 0.0)
                out[tile] = out[tile] + window[:, :LANES]
                if inner + n_local > LANES:
                    out[tile + 1] = out[tile + 1] + window[:, LANES:]
            for k in range(lat_count * n_local // LANES):
                quad_out[rank, own, k * LANES : (k + 1) * LANES] = out[k].astype(bf16)
            return inner_carry

        lax.fori_loop(0, m_local // 16, some_rows, 0)
        return carry

    own_copy = pltpu.make_async_copy(quad_out.at[0], quad_in.at[t], own_sem)

    def send_packed(rank, carry):
        @pl.when((rank == 0) & (g == 0))
        def _():
            own_copy.start()

        @pl.when((rank != 0) | (g != 0))
        def _():
            remote(
                quad_out.at[rank],
                quad_in.at[t],
                quad_send.at[rank],
                quad_recv.at[t],
                {"lat": shifted(t, distance(rank) + g, lats)},
            ).start()

        return carry

    def pass_on(rank, carry):
        s = source(rank, g)

        @pl.when((rank == 0) & (g == 0))
        def _():
            own_copy.wait()

        @pl.when((rank != 0) | (g != 0))
        def _():
            landed(quad_in.at[s], quad_recv.at[s])

        remote(
            quad_in.at[s], quad_in.at[s], beside_send.at[rank], pass_recv.at[s], {"grp": beside}
        ).start()
        remote(
            quad_in.at[s], quad_in.at[s], across_send.at[rank], pass_recv.at[s], {"grp": across}
        ).start()
        return carry

    def pass_again(rank, carry):
        s = source(rank, across)
        landed(quad_in.at[s], pass_recv.at[s])
        remote(
            quad_in.at[s], quad_in.at[s], again_send.at[rank], pass_recv.at[s], {"grp": beside}
        ).start()
        return carry

    fetches[3].wait()
    lax.fori_loop(0, turns // 2, pack, 0)
    pl.semaphore_wait(pltpu.get_barrier_semaphore(), awaited)

    @pl.when(g == 0)
    def _():
        for d in range(1, lats):
            remote(
                stage,
                sea_ref.at[y, tt],
                sea1_send.at[d],
                sea1_recv.at[tt],
                {"grp": sea_owner, "lat": shifted(t, d, lats)},
            ).start()

    @pl.when((g == 0) & (sea_owner != 0))
    def _():
        remote(
            stage, sea_ref.at[y, tt], sea1_send.at[0], sea1_recv.at[tt], {"grp": sea_owner}
        ).start()

    @pl.when((g == 0) & (sea_owner == 0))
    def _():
        sea_ref[y, tt] = stage[...]

    lax.fori_loop(0, turns // 2, send_packed, 0)
    lax.fori_loop(turns // 2, turns, pack, 0)
    lax.fori_loop(turns // 2, turns, send_packed, 0)

    for fetch in fetches[:3]:
        fetch.wait()
    tiles = line // LANES
    raw = jnp.concatenate([aloft_raw_ref[l].astype(f32) for l in range(levels)], axis=0)
    source_id = lax.broadcasted_iota(i32, (lon_local, 8 * BLK_PAD), 0)
    target_id = lax.broadcasted_iota(i32, (lon_local, 8 * BLK_PAD), 1)
    target_block, target_slot = target_id % BLK_PAD, target_id // BLK_PAD
    sorting = jnp.where(
        (target_block < blocks)
        & (target_slot < block_air)
        & (source_id == target_block * block_air + target_slot),
        1.0,
        0.0,
    ).astype(bf16)
    by_slot = jnp.dot(raw.astype(bf16), sorting, preferred_element_type=f32)
    aloft_ref[...] = jnp.zeros_like(aloft_ref)
    out_lane = lax.broadcasted_iota(i32, (8, LANES), 1)
    out_row = lax.broadcasted_iota(i32, (8, LANES), 0)
    for l in range(levels):
        for q in range(block_air):
            k = q // 2
            two = by_slot[8 * l : 8 * l + 8, k * LANES : (k + 1) * LANES]
            other = pltpu.roll(two, BLK_PAD, 1)
            both = jnp.where((out_lane < BLK_PAD) == (q % 2 == 0), two, other)
            for k in range(tiles):
                mine = out_row == 2 * k + out_lane // BLK_PAD
                aloft_ref[8 * l + q : 8 * l + q + 1, k * LANES : (k + 1) * LANES] = jnp.sum(
                    jnp.where(mine, both, 0.0), axis=0, keepdims=True
                )
    lane = lax.broadcasted_iota(i32, (8, line), 1)
    slot = lax.broadcasted_iota(i32, (8, line), 0)
    block = lane % BLK_PAD
    limit = jnp.zeros((8, line), i32)
    for i in range(lat_count):
        limit = jnp.where(lane // BLK_PAD == i, nodes_ref[i], limit)
    live = (block < blocks) & (slot < block_air)
    live = live & (y * lon_local + block * block_air + slot < limit)
    flux_sum = share_ref[0] * aloft_ref[0:8, :]
    for l in range(1, levels):
        flux_sum = flux_sum + share_ref[l] * aloft_ref[8 * l : 8 * l + 8, :]
    flux_sum = jnp.where(live, flux_sum, 0.0)
    for k in range(tiles):
        part[8 * k : 8 * k + 8, :] = flux_sum[:, k * LANES : (k + 1) * LANES]

    @pl.when(g != flux_owner)
    def _():
        remote(
            part, gathered.at[g], flux0_send, flux0_recv.at[g], {"grp": flux_owner}
        ).start()

    for r in range(lat_per):
        nearest = (t - g + lats) // grps
        k = lax.rem(nearest + lats + ((r + 1) // 2 if r % 2 else -(r // 2)), lat_per)

        @pl.when((g != 0) | (k * grps + g != t))
        def _():
            landed(sea_ref.at[y, k], sea1_recv.at[k])

        for d in range(1, lons):
            remote(
                sea_ref.at[y, k],
                sea_ref.at[y, k],
                sea2_send.at[d * lat_per + r],
                sea2_recv.at[y * lat_per + k],
                {"lon": shifted(y, d, lons)},
            ).start()

    for level in range(olev):
        ext[level, mid_rows, mid_cols] = heat_ref[level]
    wet_mid = water_ref[...].astype(f32)
    ext[olev, mid_rows, mid_cols] = wet_mid

    def tables(i, carry):
        count = jnp.full((8, LANES), nodes_ref[i], i32).astype(f32)
        inverse = jnp.concatenate([1.0 / count] * lons, axis=1)
        count = jnp.concatenate([count] * lons, axis=1)
        lane = lax.broadcasted_iota(i32, (8, wide), 1)
        row_f = lax.broadcasted_iota(i32, (8, wide), 0).astype(f32)
        inner = lane % LANES
        wave_f = ((lane // LANES) * m_local + inner).astype(f32)
        base_f = (y * lon_local).astype(f32)
        high = turn((base_f + 8 * block_air * row_f) * wave_f, count, inverse)
        low = turn((block_air * row_f) * wave_f, count, inverse)
        fine = turn(row_f * wave_f, count, inverse)
        usable = (inner < m_local) & (2.0 * wave_f < count)
        own = pl.ds(pl.multiple_of(i * 8, 8), 8)
        e2_ref[own, :wide] = jnp.where(usable, fine[0] * inverse, 0.0)
        e2_ref[own, wide:] = jnp.where(usable, fine[1] * inverse, 0.0)
        for pair in range(BLK_PAD // 16):
            real, imag = [], []
            for b in (2 * pair, 2 * pair + 1):
                hr, hi = high[0][b : b + 1], high[1][b : b + 1]
                real.append(hr * low[0] - hi * low[1])
                imag.append(hr * low[1] + hi * low[0])
            where = pl.ds(pl.multiple_of(i * BLK_PAD + pair * 16, 16), 16)
            e1_ref[where, :wide] = jnp.concatenate(real, axis=0).astype(bf16)
            e1_ref[where, wide:] = jnp.concatenate(imag, axis=0).astype(bf16)
        return carry

    lax.fori_loop(0, lat_count // 2, tables, 0)

    @pl.when(g == flux_owner)
    def _():
        gathered[g] = part[...]
        for d in range(1, grps):
            other = shifted(g, d, grps)
            landed(gathered.at[other], flux0_recv.at[other])
        total = gathered[0]
        for other in range(1, grps):
            total = total + gathered[other]
        flux_ref[t, yy] = total.astype(bf16)
        for d in range(1, lons):
            remote(
                flux_ref.at[t, yy],
                flux_ref.at[t, yy],
                flux1_send.at[d],
                flux1_recv.at[yy],
                {"lon": shifted(y, d, lons)},
            ).start()

    lax.fori_loop(lat_count // 2, lat_count, tables, 0)

    picks = 2 * blocks
    fill = jnp.zeros((picks, 8 - block_air, LANES), f32)
    fetches[5].wait()

    def prepare(i, carry):
        factor = warm_ref[pl.ds(i * picks, picks)].astype(f32)
        factor = jnp.concatenate([factor, fill], axis=1).reshape(picks * 8, LANES)
        warm_rows[i] = factor.astype(bf16)
        return carry

    lax.fori_loop(0, lat_count, prepare, 0)
    warm_ids_ref[...] = jnp.full_like(warm_ids_ref, -1)
    for i in range(lat_count):
        for k in range(warm_raw_ref.shape[1]):
            warm_ids_ref[i : i + 1, k * BLK_PAD : k * BLK_PAD + blocks] = warm_raw_ref[
                i, k : k + 1, :
            ]
    chosen = warm_ids_ref[...]
    column, row = chosen % lons, chosen // lons
    band = row // rows
    spot = (band // grps) * rows + row % rows
    spot = jnp.where((band % grps == g) & (chosen >= 0), spot + column * LANES, -1)
    spot = jnp.concatenate([spot[i : i + 1] for i in range(lat_count)], axis=1)
    table_row = lax.broadcasted_iota(i32, (LANES, lat_count * LANES), 0)

    lax.fori_loop(0, turns // 2, pass_on, 0)

    def pick_chunk(r, carry):
        other = lax.rem(y + lons + jnp.where(r % 2 == 1, (r + 1) // 2, -(r // 2)), lons)

        @pl.when(other != y)
        def _():
            for k in range(lat_per):
                landed(sea_ref.at[other, k], sea2_recv.at[other * lat_per + k])

        chunk = jnp.transpose(sea_ref[other].reshape(LANES, cols).astype(f32)).astype(bf16)
        one_hot = jnp.where(table_row == spot - other * LANES, 1.0, 0.0).astype(bf16)
        found = jnp.dot(chunk, one_hot, preferred_element_type=f32)
        picked_ref[...] = jnp.where(r == 0, found, picked_ref[...] + found)
        return carry

    picked_ref[...] = jnp.zeros_like(picked_ref)
    lax.fori_loop(0, lons, pick_chunk, 0)
    pick_id = lax.broadcasted_iota(i32, (picks, 8, LANES), 0)
    pick_lane = lax.broadcasted_iota(i32, (picks, 8, LANES), 2)
    diagonal = pick_lane == (pick_id % 2) * BLK_PAD + pick_id // 2
    warm_sums = []
    for i in range(lat_count):
        picked = picked_ref[:, i * LANES : (i + 1) * LANES].astype(bf16)
        product = jnp.dot(warm_rows[i], picked, preferred_element_type=f32)
        product = product.reshape(picks, 8, LANES)
        total = jnp.sum(jnp.where(diagonal, product, 0.0), axis=0)
        warm_sums.append(total + pltpu.roll(total, BLK_PAD, 1))
    for k in range(tiles):
        warmth_out[:, k * LANES : (k + 1) * LANES] = jnp.where(
            out_lane < BLK_PAD, warm_sums[2 * k], warm_sums[2 * k + 1]
        )
    for d in range(1, grps):
        remote(
            warmth_out,
            warmth_in.at[g],
            warmth_send.at[d],
            warmth_recv.at[g],
            {"grp": shifted(g, d, grps)},
        ).start()

    for k in range(lon_per):
        @pl.when(g * lon_per + k != y)
        def _():
            landed(flux_ref.at[t, k], flux1_recv.at[k])

    for d in range(1, lats):
        remote(
            flux_ref.at[t],
            flux_ref.at[t],
            flux2_send.at[d],
            flux2_recv.at[t],
            {"lat": shifted(t, d, lats)},
        ).start()

    def transform(field, count, out_ref):
        lane = lax.broadcasted_iota(i32, field.shape, 1)
        stacked = jnp.concatenate(
            [jnp.where(lane // BLK_PAD == i, field, 0.0) for i in range(lat_count)], axis=0
        ).astype(bf16)
        real = jnp.dot(stacked, e1_ref[:, :wide], preferred_element_type=f32)
        imag = jnp.dot(stacked, e1_ref[:, wide:], preferred_element_type=f32)
        for i in range(lat_count):
            slot_r = e2_ref[8 * i : 8 * i + 8, :wide]
            slot_i = e2_ref[8 * i : 8 * i + 8, wide:]
            for l in range(count):
                at = (i * count + l) * 8
                re, im = real[at : at + 8], imag[at : at + 8]
                out_r = jnp.sum(re * slot_r - im * slot_i, axis=0, keepdims=True)
                out_i = jnp.sum(re * slot_i + im * slot_r, axis=0, keepdims=True)
                for c, out in enumerate((out_r, out_i)):
                    row = (2 * l + c) * lat_count + i
                    for k in range(lons):
                        out_ref[k, row : row + 1, :] = out[:, k * LANES : (k + 1) * LANES]

    transform(
        jnp.concatenate(
            [jnp.where(live, aloft_ref[8 * l : 8 * l + 8, :], 0.0) for l in range(levels)], axis=0
        ),
        levels,
        waves,
    )
    lax.fori_loop(turns // 2, turns, pass_on, 0)
    warmth = warmth_out[...]
    for d in range(1, grps):
        other = shifted(g, d, grps)
        landed(warmth_in.at[other], warmth_recv.at[other])
        warmth = warmth + warmth_in[other]
    transform(jnp.where(live, warmth, 0.0), 1, sea_waves)
    for l in range(levels):
        at = slice(2 * l * lat_count, 2 * (l + 1) * lat_count)
        waves[:, at, :] = waves[:, at, :] + sens_ref[l] * sea_waves[...]
    waves_out[...] = waves[...].astype(bf16)
    for d in range(1, lons):
        other = shifted(y, d, lons)
        remote(
            waves_out.at[other],
            waves_in.at[y],
            waves_send.at[d],
            waves_recv.at[y],
            {"lon": other},
        ).start()

    for d in range(1, lats):
        other = shifted(t, d, lats)
        landed(flux_ref.at[other], flux2_recv.at[other])
    ways = cool_raw_ref.shape[0]
    for k in range(ways):
        cool_ids_ref[0:1, k * rows : (k + 1) * rows] = cool_raw_ref[k : k + 1, :]
    chosen = cool_ids_ref[0:1, :]
    parallel, place = chosen // (blocks * lons), chosen % (blocks * lons)
    band, within = parallel // lat_count, parallel % lat_count
    lon, blk = place // blocks, place % blocks
    group = (band * lon_per + lon % lon_per) * tiles + within // 2
    group = jnp.where(lon // lon_per == g, group, -1)
    spot = (within % 2) * BLK_PAD + blk
    group_count = lats * lon_per * tiles
    one_hot = jnp.where(
        lax.broadcasted_iota(i32, (LANES, LANES), 0) == spot, 1.0, 0.0
    ).astype(bf16)
    found = jnp.dot(
        flux_ref[...].reshape(group_count * 8, LANES), one_hot, preferred_element_type=f32
    ).reshape(group_count, 8, LANES)
    group_id = lax.broadcasted_iota(i32, (group_count, 8, LANES), 0)
    air = jnp.sum(jnp.where(group_id == group[None], found, 0.0), axis=0)
    width = rows * block_air * 8
    to = lax.broadcasted_iota(i32, (LANES, width), 1)
    repeat = jnp.where(
        (to % 8 < ways)
        & (lax.broadcasted_iota(i32, (LANES, width), 0) == (to % 8) * rows + to // (8 * block_air)),
        1.0,
        0.0,
    ).astype(bf16)
    air = jnp.dot(air.astype(bf16), repeat, preferred_element_type=f32)
    to = lax.broadcasted_iota(i32, (8, width), 1)
    own_slot = (to // 8) % block_air == lax.broadcasted_iota(i32, (8, width), 0)
    air = jnp.sum(jnp.where(own_slot, air, 0.0), axis=0, keepdims=True)
    air = jnp.where(
        lax.broadcasted_iota(i32, (rows, width), 1) // (8 * block_air)
        == lax.broadcasted_iota(i32, (rows, width), 0),
        air,
        0.0,
    ).astype(bf16)
    fetches[4].wait()
    factor = cool_ref[...].astype(f32)
    factor = jnp.concatenate(
        [factor, jnp.zeros((rows * block_air, 8 - ways, LANES), f32)], axis=1
    ).reshape(width, LANES)
    flux_out[...] = jnp.dot(air, factor.astype(bf16), preferred_element_type=f32)

    @pl.when(g != 0)
    def _():
        remote(
            flux_out, flux_in.at[g], fluxp_send, fluxp_recv.at[g], {"grp": jnp.int32(0)}
        ).start()

    lax.fori_loop(0, turns // 2, pass_again, 0)

    total = waves[y]
    for d in range(1, lons):
        other = shifted(y, d, lons)
        landed(waves_in.at[other], waves_recv.at[other])
        total = total + waves_in[other].astype(f32)
    fourier[t] = total.astype(bf16)

    def send_fourier(offset):
        @pl.when(offset != 0)
        def _():
            remote(
                fourier.at[t],
                fourier.at[t],
                fourier_send.at[offset],
                fourier_recv.at[t],
                {"lat": shifted(t, offset, lats)},
            ).start()

    def send_some(rank, carry):
        for member in range(grps):
            send_fourier(distance(rank) + member)
        return carry

    lax.fori_loop(0, turns, send_some, 0)

    lax.fori_loop(turns // 2, turns, pass_again, 0)

    @pl.when(g == 0)
    def _():
        total = flux_out[...]
        for other in range(1, grps):
            landed(flux_in.at[other], fluxp_recv.at[other])
            total = total + flux_in[other]
        ext[0, mid_rows, mid_cols] = heat_ref[0] + FLUX_RATE * total * wet_mid

    for index, (partner, src_rows, dst_rows, dst_cols) in enumerate(halo):
        remote(
            ext.at[:, src_rows, mid_cols],
            ext.at[:, dst_rows, dst_cols],
            halo_send.at[index],
            halo_recv.at[index],
            partner,
        ).start()


    span = lat_count * n_local
    repeat_row = lax.broadcasted_iota(i32, (LANES, span), 0)
    repeat = jnp.where(
        (repeat_row < parts * lat_count)
        & (repeat_row % lat_count == lax.broadcasted_iota(i32, (LANES, span), 1) // n_local),
        1.0,
        0.0,
    ).astype(bf16)
    fill = jnp.zeros((LANES - parts * lat_count, LANES), f32)
    part_lane = lax.broadcasted_iota(i32, (m_local, LANES), 1) // lat_count
    sums[...] = jnp.zeros_like(sums)

    def coefficients(s):
        @pl.when(s != t)
        def _():
            landed(fourier.at[s], fourier_recv.at[s])

        columns = jnp.transpose(jnp.concatenate([fourier[s].astype(f32), fill], axis=0))[:m_local]
        own = jnp.concatenate(
            [jnp.where(part_lane == a, columns, 0.0) for a in range(parts)], axis=0
        ).astype(bf16)
        return jnp.dot(own, repeat, preferred_element_type=f32)

    def add_two(first, second):
        coefs = coefficients(first), coefficients(second)
        quads = quad_in[first].astype(f32), quad_in[second].astype(f32)
        for a in range(parts):
            at = slice(a * m_local, (a + 1) * m_local)
            sums[at, :] = sums[at, :] + coefs[0][at] * quads[0] + coefs[1][at] * quads[1]

    def add_some(rank, carry):
        add_two(source(rank, g), source(rank, across))
        for member in (beside, beyond):
            s = source(rank, member)
            landed(quad_in.at[s], pass_recv.at[s])
        add_two(source(rank, beside), source(rank, beyond))
        return carry

    lax.fori_loop(0, 3 * turns // 4, add_some, 0)

    for index, (partner, src_rows, dst_rows, dst_cols) in enumerate(halo):
        landed(ext.at[:, dst_rows, dst_cols], halo_recv.at[index])
    shape = (rows + 16, cols + 2 * LANES)
    row_id = lax.broadcasted_iota(i32, shape, 0) + (t * rows - 8)
    col_id = lax.broadcasted_iota(i32, shape, 1) + (y * cols - LANES)
    inside = (row_id >= 0) & (row_id < rows * lats) & (col_id >= 0) & (col_id < cols * lons)
    wet = jnp.where(inside, ext[olev], 0.0)
    moves = ((1, 0), (shape[0] - 1, 0), (1, 1), (shape[1] - 1, 1))
    wet_near = [pltpu.roll(wet, shift, axis) for shift, axis in moves]
    for level in range(olev):
        field = ext[level]
        for _ in range(2):
            total = jnp.zeros_like(field)
            for (shift, axis), near in zip(moves, wet_near):
                total = total + near * (pltpu.roll(field, shift, axis) - field)
            field = field + KAPPA * wet * total
        ocean_ref[level] = field[mid_rows, mid_cols]

    lax.fori_loop(3 * turns // 4, turns, add_some, 0)

    folded = jnp.zeros((parts * m_local, LANES), f32)
    for i in range(lat_count):
        tile, inner = divmod(i * n_local, LANES)
        if inner + n_local > LANES:
            window = sums[:, tile * LANES : (tile + 2) * LANES]
            folded = folded + pltpu.roll(window, 2 * LANES - inner, 1)[:, :LANES]
        else:
            window = sums[:, tile * LANES : (tile + 1) * LANES]
            folded = folded + (pltpu.roll(window, LANES - inner, 1) if inner else window)
    width = spec_ref.shape[1]
    folded = jnp.concatenate(
        [folded, jnp.zeros((width - parts * m_local, LANES), f32)], axis=0
    )
    result = jnp.transpose(folded)[:n_local]
    lane = lax.broadcasted_iota(i32, result.shape, 1)
    degree = lax.broadcasted_iota(i32, result.shape, 0) + t * n_local
    spec_ref[...] = jnp.where(degree >= lane % m_local + y * m_local, result, 0.0)

    @pl.when(g == 0)
    def _():
        for d in range(1, lats):
            landed(stage, sea1_send.at[d])

    @pl.when((g == 0) & (sea_owner != 0))
    def _():
        landed(stage, sea1_send.at[0])

    @pl.when(g != flux_owner)
    def _():
        landed(part, flux0_send)

    @pl.when(g == flux_owner)
    def _():
        for d in range(1, lons):
            landed(flux_ref.at[t, yy], flux1_send.at[d])

    @pl.when(g != 0)
    def _():
        landed(flux_out, fluxp_send)

    for d in range(1, lats):
        landed(flux_ref.at[t], flux2_send.at[d])
        landed(fourier.at[t], fourier_send.at[d])
    for d in range(1, lons):
        for r in range(lat_per):
            landed(sea_ref.at[y, 0], sea2_send.at[d * lat_per + r])
        landed(waves_out.at[0], waves_send.at[d])
    for d in range(1, grps):
        landed(warmth_out, warmth_send.at[d])
    for index, (partner, src_rows, dst_rows, dst_cols) in enumerate(halo):
        landed(ext.at[:, src_rows, mid_cols], halo_send.at[index])

    def sent(rank, carry):
        @pl.when((rank != 0) | (g != 0))
        def _():
            landed(quad_out.at[rank], quad_send.at[rank])

        for sem in (beside_send, across_send, again_send):
            landed(quad_in.at[0], sem.at[rank])
        return carry

    lax.fori_loop(0, turns, sent, 0)


def per_device(
    aloft_gridpoint,
    parallel_nodes,
    layer_pressure_share,
    layer_sensitivity,
    associated_polynomial_quadrature,
    marine_heat,
    water_indicator,
    heat_feeding_panels,
    heat_transfer_factors,
    skin_warmth_feeding_panels,
    skin_warmth_mapping_factors,
):
    grps, lats, lons = (lax.axis_size(name) for name in ("grp", "lat", "lon"))
    levels, lat_count, lon_local = aloft_gridpoint.shape
    block_air = heat_transfer_factors.shape[3]
    blocks = lon_local // block_air
    olev, rows, cols = marine_heat.shape
    m_local, degrees = associated_polynomial_quadrature.shape[1:]
    lon_per, lat_per = lons // grps, lats // grps
    wide = lons * LANES
    line = lat_count * BLK_PAD
    parts = 2 * levels
    n_local = degrees // lats
    width = -(-parts * m_local // LANES) * LANES
    warm_ways = skin_warmth_feeding_panels.shape[2]
    cool_ways = heat_feeding_panels.shape[2]
    vmem = pl.BlockSpec(memory_space=pltpu.VMEM)
    hbm = pl.BlockSpec(memory_space=pl.ANY)
    f32, bf16 = jnp.float32, jnp.bfloat16
    dma, dmas = pltpu.SemaphoreType.DMA, lambda n: pltpu.SemaphoreType.DMA((n,))

    warm_ids = skin_warmth_feeding_panels.transpose(0, 2, 1)
    cool_ids = heat_feeding_panels[:, 0, :].transpose(1, 0)
    cool_factors = heat_transfer_factors.transpose(0, 1, 3, 2, 4)

    sizes = (
        grps, lats, lons, lat_count, levels, lon_local, block_air, m_local, degrees, olev, rows, cols
    )
    spec, ocean = pl.pallas_call(
        functools.partial(step_kernel, sizes),
        out_shape=(
            jax.ShapeDtypeStruct((n_local, width), f32),
            jax.ShapeDtypeStruct((olev, rows, cols), f32),
        ),
        in_specs=[hbm] * 6 + [vmem] * 5,
        out_specs=(vmem, vmem),
        scratch_shapes=[
            pltpu.SMEM((lat_count,), jnp.int32),
            pltpu.SMEM((levels,), f32),
            pltpu.SMEM((levels,), f32),
            pltpu.VMEM((lat_count, m_local, degrees), bf16),
            pltpu.VMEM((lat_count * blocks * warm_ways, block_air, cols), bf16),
            pltpu.VMEM((rows * block_air, cool_ways, cols), bf16),
            pltpu.VMEM((lons, lat_per, rows, cols), bf16),
            pltpu.VMEM((lats, lon_per, line // 16, LANES), bf16),
            pltpu.VMEM((line, 2 * wide), bf16),
            pltpu.VMEM((lat_count * 8, 2 * wide), f32),
            pltpu.VMEM((lat_count, blocks * warm_ways * 8, cols), bf16),
            pltpu.VMEM((cols, lat_count * LANES), f32),
            pltpu.VMEM((levels * 8, line), f32),
            pltpu.VMEM((lat_count, warm_ways * BLK_PAD), jnp.int32),
            pltpu.VMEM((8, rows * cool_ways), jnp.int32),
            pltpu.VMEM((rows, cols), bf16),
            pltpu.VMEM((line // 16, LANES), f32),
            pltpu.VMEM((grps, line // 16, LANES), f32),
            pltpu.VMEM((8, line), f32),
            pltpu.VMEM((grps, 8, line), f32),
            pltpu.VMEM((rows, cols), f32),
            pltpu.VMEM((grps, rows, cols), f32),
            pltpu.VMEM((olev + 1, rows + 16, cols + 2 * LANES), f32),
            pltpu.VMEM((lons, 2 * lat_count, LANES), f32),
            pltpu.VMEM((lons, parts * lat_count, LANES), f32),
            pltpu.VMEM((lons, parts * lat_count, LANES), bf16),
            pltpu.VMEM((lons, parts * lat_count, LANES), bf16),
            pltpu.VMEM((lats, parts * lat_count, LANES), bf16),
            pltpu.VMEM((lats // grps, m_local, lat_count * n_local), bf16),
            pltpu.VMEM((lats, m_local, lat_count * n_local), bf16),
            pltpu.VMEM((parts * m_local, lat_count * n_local), f32),
            dmas(6),
            dma,
            dmas(lats),
            dmas(lat_per),
            dma,
            dmas(grps),
            dmas(lons),
            dmas(lon_per),
            dmas(lons * lat_per),
            dmas(lons * lat_per),
            dmas(lats),
            dmas(lats),
            dmas(grps),
            dmas(grps),
            dma,
            dmas(grps),
            dmas(8),
            dmas(8),
            dmas(lons),
            dmas(lons),
            dmas(lats),
            dmas(lats),
            dmas(lats // grps),
            dmas(lats),
            dmas(lats // grps),
            dmas(lats // grps),
            dmas(lats // grps),
            dmas(lats),
        ],
        compiler_params=pltpu.CompilerParams(
            collective_id=0, has_side_effects=True, vmem_limit_bytes=VMEM_LIMIT
        ),
    )(
        parallel_nodes,
        layer_pressure_share,
        layer_sensitivity,
        associated_polynomial_quadrature,
        skin_warmth_mapping_factors.reshape(-1, block_air, cols),
        cool_factors.reshape(-1, cool_ways, cols),
        aloft_gridpoint,
        marine_heat,
        water_indicator,
        warm_ids,
        cool_ids,
    )
    spectra = spec[:, : parts * m_local].reshape(n_local, parts, m_local)
    return (spectra, ocean)


def solution(mesh):
    in_specs = (
        P("grp", "lat", "lon"),
        P("lat"),
        P("grp"),
        P("grp"),
        P("lat", "lon", None),
        P("grp", "lat", "lon"),
        P("lat", "lon"),
        P("lat", "lon", None),
        P("lat", "lon", None, None, None),
        P("lat", "lon", None),
        P("lat", "lon", None, None, None),
    )
    out_specs = (P("lat", "grp", "lon"), P("grp", "lat", "lon"))
    return jax.shard_map(
        per_device, mesh=mesh, in_specs=in_specs, out_specs=out_specs, check_vma=False
    )
```
